256 devices in a mesh: video: 4 (over y), tm: 64 (over x, z, core).
Axes of the slice: x: 4, y: 4, z: 8, core: 2. Of those that a mesh axis runs over, the one named last changes fastest.
Arguments:
- bin_grad: bfloat16 [16, 256, 16, 1024], P('video', 'tm'), may hold values from -0.046875 to 0.046875
- tap_weight: float32 [16, 256, 16, 2], P('video', 'tm'), may hold values from 0.05 to 1
- tap_index: int32 [16, 256, 16, 2], P('video', 'tm'), may hold values from 0 to 8191, as said below
- features: bfloat16 [16, 8192, 1024], P('video', 'tm'), may hold values from -6 to 6
- preact: bfloat16 [16, 8192, 1024], P('video', 'tm'), may hold values from -8 to 8
- filter_second: bfloat16 [3, 1024, 1024], replicated, may hold values from -0.109375 to 0.109375
Outputs:
- first_filter_grad: float32 [1024, 3, 1024], P('tm')
- second_filter_grad: float32 [1024, 3, 1024], P('tm')
The draws below stay inside these ranges and needn't reach their ends.
Inputs may be any that keep to these rules, and one draw needn't show every extreme that they name: `tap_index`: each proposal spans the integer snippets a to a + L for a start a and a length L of 1 or more; the taps of bin b are a + ((2 b + 1) L) // 32 and that snippet plus one. For the proposals held by one device (its 4 videos and 4 proposals of each), at most 32 taps fall into any one block of 128 snippets (snippets 128 * m to 128 * m + 127, taken over its videos together), and exactly 32 into some block.
All inputs are finite; a program needn't handle non-finite values.
Results may differ from the reference program's by a relative error of at most 0.0048.
Values may be sent and summed in bfloat16 or wider, within the bound.
No kernel may reach another device: no remote copies, remote signals or barrier semaphores. Data moves between devices by JAX's collectives and lax.ppermute only.
A program may use at most 192 MiB of HBM per device.

```python
import jax
import jax.numpy as jnp
from jax import lax

C = 1024
BINS = 16
TAPS = 2
KERNEL = 3
V_DEV = 4
SNIP_DEV = 128
P_DEV = 4
VIDEOS = 16
SNIPS = 8192
PROPS = 256


def lane_spans(key, busiest, tm_total, lane_props):
    keys = jax.random.split(key, 6)
    peers = jnp.arange(tm_total, dtype=jnp.int32)
    forced = (peers == 0) & (busiest != 0) | (peers == busiest + 1)
    eligible = (peers != busiest) & jnp.logical_not(forced)
    ranking = jax.random.permutation(keys[0], tm_total).astype(jnp.int32)
    priority = jnp.where(forced, 2 * tm_total + peers, jnp.where(eligible, ranking, -1 - peers))
    unused, picked = lax.top_k(priority, lane_props - 1)
    begin = jnp.sort(picked.astype(jnp.int32))
    after = jnp.concatenate([begin[1:], jnp.full((1,), tm_total, jnp.int32)])
    limit = jnp.where(busiest > begin, busiest, tm_total)
    finish = jnp.minimum(after, limit)
    lowest = begin * SNIP_DEV
    span = (finish - begin) * SNIP_DEV
    shape = (lane_props - 1,)
    longest = jax.random.randint(keys[1], shape, 1, span).astype(jnp.int32)
    length = jax.random.randint(keys[2], shape, 1, longest + 1).astype(jnp.int32)
    start = lowest + jax.random.randint(keys[3], shape, 0, span - length).astype(jnp.int32)
    short_len = jax.random.randint(keys[4], (1,), 1, SNIP_DEV).astype(jnp.int32)
    short_start = busiest * SNIP_DEV + jax.random.randint(keys[5], (1,), 0, SNIP_DEV - short_len).astype(jnp.int32)
    return (jnp.concatenate([short_start, start]), jnp.concatenate([short_len, length]))


def device_taps(key, tm_total):
    prop_total = V_DEV * P_DEV
    lane_total = (prop_total + tm_total - 1) // tm_total
    lane_props = prop_total // lane_total
    key_busy, key_lanes, key_mix = jax.random.split(key, 3)
    busiest = jax.random.randint(key_busy, (), 0, tm_total).astype(jnp.int32)
    lane_keys = jax.random.split(key_lanes, lane_total)
    starts, lengths = jax.vmap(lambda single: lane_spans(single, busiest, tm_total, lane_props))(lane_keys)
    order = jax.random.permutation(key_mix, prop_total)
    starts = starts.reshape(prop_total)[order]
    lengths = lengths.reshape(prop_total)[order]
    centre = 2 * jnp.arange(BINS, dtype=jnp.int32) + 1
    first = starts[:, None] + centre[None, :] * lengths[:, None] // (2 * BINS)
    taps = jnp.stack([first, first + 1], axis=-1)
    return taps.reshape(V_DEV, P_DEV, BINS, TAPS).astype(jnp.int32)


def draw_tap_index(key, part):
    key = jax.random.fold_in(key, 7)
    video_total = VIDEOS // V_DEV
    tm_total = PROPS // P_DEV
    keys = jax.random.split(key, video_total * tm_total)
    blocks = jax.vmap(lambda single: device_taps(single, tm_total))(keys)
    blocks = blocks.reshape(video_total, tm_total, V_DEV, P_DEV, BINS, TAPS).transpose(0, 2, 1, 3, 4, 5)
    return blocks.reshape(VIDEOS, PROPS, BINS, TAPS).astype(jnp.int32)


def steps_of(rng, extent, cuts, least, high):
    factor_of = 1.0
    for position, shards_of in cuts:
        draws = jax.random.uniform(jax.random.fold_in(jax.random.fold_in(rng, 6), position), (shards_of,), jnp.float32, least / len(cuts), high / len(cuts))
        factor_of = factor_of * jnp.repeat(jnp.exp(draws), extent[position] // shards_of).reshape((-1,) + (1,) * (len(extent) - 1 - position))
    return factor_of


def scatter_about(stream_key, dims, spread, most, cuts=(), kind=jnp.bfloat16):
    drawn = spread * jax.random.normal(stream_key, dims, jnp.float32)
    if cuts:
        drawn = drawn * steps_of(stream_key, dims, cuts, -0.22, 0.18)
    return jnp.clip(drawn, -most, most).astype(kind)


def setup_inputs(seed: int = 0) -> dict:
    arg_keys = jax.random.split(jax.random.key(seed), 7)
    bin_grad = scatter_about(arg_keys[0], (VIDEOS, PROPS, BINS, C), (3.0 / (VIDEOS * SNIPS) ** 0.5), 0.046875, ((0, 4), (1, 64)))
    tap_weight = jnp.clip(0.05 + 0.95 * jax.random.uniform(arg_keys[1], (VIDEOS, PROPS, BINS, TAPS), jnp.float32) ** steps_of(arg_keys[1], (VIDEOS, PROPS, BINS, TAPS), ((0, 4), (1, 64)), -0.2, 0.2), 0.05, 1.0)
    tap_index = draw_tap_index(jax.random.fold_in(arg_keys[6], 71), 0)
    features = scatter_about(arg_keys[3], (VIDEOS, SNIPS, C), 1.0, 6.0, ((0, 4), (1, 64)))
    preact = scatter_about(arg_keys[4], (VIDEOS, SNIPS, C), 1.5, 8.0, ((0, 4), (1, 64)))
    filter_second = scatter_about(arg_keys[5], (KERNEL, C, C), (KERNEL * C) ** -0.5, 0.109375)
    return dict(bin_grad=bin_grad, tap_weight=tap_weight, tap_index=tap_index, features=features, preact=preact, filter_second=filter_second)


def silu_slope(values):
    sigma = jax.nn.sigmoid(values)
    return sigma * (1.0 + values * (1.0 - sigma))

def filter_grad(inputs, gradients):
    padded = jnp.pad(inputs, ((0, 0), (1, 1), (0, 0)))
    blocks = []
    for lag_index in range(KERNEL):
        window = padded[:, lag_index:lag_index + SNIPS, :].reshape(-1, C)
        blocks.append(jnp.dot(window.T, gradients, preferred_element_type=jnp.float32))
    return jnp.stack(blocks, axis=1)

def reference(bin_grad, tap_weight, tap_index, features, preact, filter_second):
    scaled = (tap_weight[..., None] * bin_grad[:, :, :, None, :].astype(jnp.float32)).astype(jnp.bfloat16)
    video_of = lax.broadcasted_iota(jnp.int32, tap_index.shape, 0)
    segment = (video_of * SNIPS + tap_index).reshape(-1).astype(jnp.int32)
    summed = jax.ops.segment_sum(scaled.reshape(-1, C).astype(jnp.float32), segment, num_segments=VIDEOS * SNIPS)
    snippet_grad = summed.astype(jnp.bfloat16).reshape(VIDEOS, SNIPS, C)
    pre_values = preact.astype(jnp.float32)
    activation = jax.nn.silu(pre_values).astype(jnp.bfloat16)
    grad_padded = jnp.pad(snippet_grad, ((0, 0), (1, 1), (0, 0)))
    act_grad = jnp.zeros((VIDEOS * SNIPS, C), jnp.float32)
    for lag_index in range(KERNEL):
        window = grad_padded[:, 2 - lag_index:2 - lag_index + SNIPS, :].reshape(-1, C)
        act_grad = act_grad + jnp.dot(window, filter_second[lag_index].T, preferred_element_type=jnp.float32)
    pre_grad = (act_grad * silu_slope(pre_values.reshape(-1, C))).astype(jnp.bfloat16)
    first = filter_grad(features, pre_grad)
    second = filter_grad(activation, snippet_grad.reshape(-1, C))
    return (first, second)
```

```python
import jax
import jax.numpy as jnp
import numpy as np
from jax import lax
from jax.sharding import Mesh
from jax.sharding import PartitionSpec as P

TM = ("x", "z", "core")
TM_SIZES = (4, 8, 2)
META = 128


def silu_slope(values):
    sigma = jax.nn.sigmoid(values)
    return sigma * (1.0 + values * (1.0 - sigma))


def neighbours(value, forward):
    count = lax.axis_size(TM)
    pairs = [(i, i + 1) for i in range(count - 1)]
    if not forward:
        pairs = [(j, i) for i, j in pairs]
    return lax.ppermute(value, TM, pairs)


def ring_shift(value, axis, shift):
    count = lax.axis_size(axis)
    return lax.ppermute(value, axis, [(i, (i + shift) % count) for i in range(count)])


def exchange(value, axis):
    return lax.all_to_all(value, axis, split_axis=0, concat_axis=0, tiled=True)


def route(first_tap, snip_count, unit_axis):
    count = first_tap[0].shape[0]
    col, row = first_tap
    mine, other = (col, row) if unit_axis == 0 else (row, col)
    reduce_axis = 1 - unit_axis
    block, block_other = mine // snip_count, other // snip_count
    crossing = mine % snip_count == snip_count - 1
    crossing_other = other % snip_count == snip_count - 1
    earlier = lax.broadcasted_iota(jnp.int32, (count, count), reduce_axis) < lax.broadcasted_iota(
        jnp.int32, (count, count), unit_axis
    )
    rank = jnp.sum(
        ((block == block_other) & crossing_other & earlier).astype(jnp.int32),
        axis=reduce_axis,
        keepdims=True,
    )
    target = block + (crossing & (rank % 2 == 1)).astype(jnp.int32)
    return target, mine - target * snip_count


def halved(value):
    high = lax.reduce_precision(value, 8, 7)
    rest = value - high
    middle = lax.reduce_precision(rest, 8, 7)
    return high, middle, rest - middle


def send_slots(bin_grad, tap_weight, tap_index, snip_count, peers):
    video_count, prop_count, bin_count, tap_count = tap_index.shape
    channels = bin_grad.shape[-1]
    units = video_count * prop_count * bin_count
    capacity = bin_count * ((video_count * prop_count + peers - 1) // peers)
    first = tap_index[..., 0].reshape(units)
    taps = (first[:, None], first[None, :])
    target_col, local = route(taps, snip_count, 0)
    target_row, _ = route(taps, snip_count, 1)
    earlier = lax.broadcasted_iota(jnp.int32, (units, units), 0) < lax.broadcasted_iota(
        jnp.int32, (units, units), 1
    )
    position = jnp.sum(
        ((target_col == target_row) & earlier).astype(jnp.int32), axis=0, keepdims=True
    )
    slot = target_row * capacity + position
    matches = (
        lax.broadcasted_iota(jnp.int32, (peers * capacity, units), 0) == slot
    ).astype(jnp.bfloat16)
    video = lax.broadcasted_iota(jnp.int32, (units, 1), 0) // (prop_count * bin_count)
    main = video_count * snip_count

    def line(step):
        at = local + step
        inside = video * snip_count + at
        edge = main + video + jnp.where(at < 0, 0, video_count)
        return jnp.where((at < 0) | (at >= snip_count), edge, inside)

    weights = tap_weight.reshape(units, tap_count)
    columns = []
    for step in range(2):
        where_to = line(step)
        columns += [(where_to // 256).astype(jnp.float32), (where_to % 256).astype(jnp.float32)]
        columns += list(halved(weights[:, step : step + 1]))
    lane = lax.broadcasted_iota(jnp.int32, (units, META), 1)
    meta = jnp.zeros((units, META), jnp.float32)
    for index, column in enumerate(columns):
        meta = jnp.where(lane == index, column, meta)
    payload = jnp.concatenate([bin_grad.reshape(units, channels), meta.astype(jnp.bfloat16)], axis=1)
    rows = jnp.dot(matches, payload, preferred_element_type=jnp.float32).astype(jnp.bfloat16)
    return rows.reshape(peers, capacity, channels + META)


def collect(got, channels, row_count):
    rows = got.reshape(-1, channels + META)
    grads = rows[:, :channels].astype(jnp.float32)
    meta = rows[:, channels:].astype(jnp.float32)
    meta_t = meta[:, :16].T
    total = jnp.zeros((row_count, channels), jnp.float32)
    for step in range(2):
        base = 5 * step
        where_to = (meta_t[base : base + 1] * 256.0 + meta_t[base + 1 : base + 2]).astype(jnp.int32)
        weight = meta[:, base + 2 : base + 3] + meta[:, base + 3 : base + 4] + meta[:, base + 4 : base + 5]
        tap_rows = (weight * grads).astype(jnp.bfloat16)
        table = (
            lax.broadcasted_iota(jnp.int32, (row_count, rows.shape[0]), 0) == where_to
        ).astype(jnp.bfloat16)
        total = total + jnp.dot(table, tap_rows, preferred_element_type=jnp.float32)
    return total


def shifted(main, low, high):
    before = jnp.concatenate([low, main[..., :-1, :]], axis=-2)
    after = jnp.concatenate([main[..., 1:, :], high], axis=-2)
    return before, after


def input_windows(shard, low, high):
    video_count, snip_count, channels = shard.shape
    block = jnp.concatenate([shard.reshape(-1, channels), low, high], axis=0)
    every = lax.all_gather(block, "video", axis=0, tiled=False)
    main_rows = video_count * snip_count
    main = every[:, :main_rows].reshape(-1, video_count, snip_count, channels)
    low_all = every[:, main_rows : main_rows + video_count][:, :, None, :]
    high_all = every[:, main_rows + video_count :][:, :, None, :]
    before, after = shifted(main, low_all, high_all)
    return [part.reshape(-1, channels) for part in (before, main, after)]


def to_quarters(gradient, channels):
    count = lax.axis_size("video")
    rows = gradient.shape[0]
    parts = gradient.reshape(rows, count, channels // count).transpose(1, 0, 2)
    return exchange(parts, "video").reshape(count * rows, channels // count)


def filter_terms(windows, gradient):
    blocks = [
        lax.dot_general(
            window, gradient, (((0,), (0,)), ((), ())), preferred_element_type=jnp.float32
        )
        for window in windows
    ]
    return jnp.stack(blocks, axis=0)


def reduce_core_x(terms):
    x_total, z_total, cores = (lax.axis_size(name) for name in TM)
    lags, channels, outs = terms.shape
    each = channels // (x_total * z_total * cores)
    parts = terms.reshape(lags, x_total, z_total, cores, each, outs).transpose(3, 1, 2, 0, 4, 5)
    core = lax.axis_index("core")
    keep = lax.dynamic_index_in_dim(parts, core, 0, keepdims=False)
    give = lax.dynamic_index_in_dim(parts, 1 - core, 0, keepdims=False).astype(jnp.bfloat16)
    got = ring_shift(give, "core", 1)
    share = (keep + got.astype(jnp.float32)).astype(jnp.bfloat16)
    share = exchange(share.reshape(x_total, z_total * lags * each, outs), "x")
    return jnp.sum(share.astype(jnp.float32), axis=0).reshape(z_total, lags * each, outs)


def on_device(bin_grad, tap_weight, tap_index, features, preact, filter_second):
    video_count, snip_count, channels = features.shape
    peers = lax.axis_size(TM)
    main_rows = video_count * snip_count
    sent = send_slots(bin_grad, tap_weight, tap_index, snip_count, peers)
    got = exchange(sent, TM)

    pre_values = preact.astype(jnp.float32)
    activation = jax.nn.silu(pre_values).astype(jnp.bfloat16)
    edge_low = neighbours(jnp.concatenate([activation[:, -1], features[:, -1]], axis=0), True)
    edge_high = neighbours(jnp.concatenate([activation[:, 0], features[:, 0]], axis=0), False)
    act_windows = input_windows(activation, edge_low[:video_count], edge_high[:video_count])
    feature_windows = input_windows(features, edge_low[video_count:], edge_high[video_count:])

    partial = collect(got, channels, main_rows + 2 * video_count)
    main = partial[:main_rows].reshape(video_count, snip_count, channels)
    low = partial[main_rows : main_rows + video_count]
    high = partial[main_rows + video_count :]
    from_low = neighbours(jnp.stack([main[:, -1], high]), True)
    from_high = neighbours(jnp.stack([low, main[:, 0]]), False)
    row = lax.broadcasted_iota(jnp.int32, main.shape, 1)
    main = main + jnp.where(row == 0, from_low[1][:, None], 0.0)
    main = main + jnp.where(row == snip_count - 1, from_high[0][:, None], 0.0)
    snippet_grad = main.astype(jnp.bfloat16)
    low = (low + from_low[0]).astype(jnp.bfloat16)[:, None]
    high = (high + from_high[1]).astype(jnp.bfloat16)[:, None]
    before, after = shifted(snippet_grad, low, high)

    snippet_rows = snippet_grad.reshape(main_rows, channels)
    snippet_share = to_quarters(snippet_rows, channels)

    act_grad = jnp.zeros((main_rows, channels), jnp.float32)
    for window, taps in zip((after, snippet_grad, before), filter_second):
        act_grad = act_grad + lax.dot_general(
            window.reshape(main_rows, channels),
            taps,
            (((1,), (1,)), ((), ())),
            preferred_element_type=jnp.float32,
        )
    pre_grad = (act_grad * silu_slope(pre_values.reshape(-1, channels))).astype(jnp.bfloat16)
    pre_share = to_quarters(pre_grad, channels)

    second = reduce_core_x(filter_terms(act_windows, snippet_share))
    first = reduce_core_x(filter_terms(feature_windows, pre_share))
    both = jnp.concatenate([first, second], axis=1).astype(jnp.bfloat16)
    mine = jnp.sum(exchange(both, "z").astype(jnp.float32), axis=0)

    quarters = lax.axis_size("video")
    place = lax.axis_index("video")
    held = [mine] + [ring_shift(mine, "video", shift) for shift in range(1, quarters)]
    blocks = []
    for quarter in range(quarters):
        block = held[0]
        for shift in range(1, quarters):
            block = jnp.where((place - shift) % quarters == quarter, held[shift], block)
        blocks.append(block)
    whole = jnp.concatenate(blocks, axis=-1)
    lags = filter_second.shape[0]
    whole = whole.reshape(2, lags, -1, channels).transpose(0, 2, 1, 3)
    return (whole[0], whole[1])


def solution(mesh):
    shape = (mesh.shape["video"],) + TM_SIZES
    fine = Mesh(np.asarray(mesh.devices).reshape(shape), ("video",) + TM)
    return jax.shard_map(
        on_device,
        mesh=fine,
        in_specs=(
            P("video", TM, None, None),
            P("video", TM, None, None),
            P("video", TM, None, None),
            P("video", TM, None),
            P("video", TM, None),
            P(),
        ),
        out_specs=(P(TM, None, None), P(TM, None, None)),
        check_vma=False,
    )
```

```python
import jax
import jax.numpy as jnp
import numpy as np
from jax import lax
from jax.experimental import pallas as pl
from jax.experimental.pallas import tpu as pltpu
from jax.sharding import Mesh
from jax.sharding import PartitionSpec as P

TM = ("x", "z", "core")
TM_SIZES = (4, 8, 2)
META = 128


def silu_slope(values):
    sigma = jax.nn.sigmoid(values)
    return sigma * (1.0 + values * (1.0 - sigma))


def neighbours(value, forward):
    count = lax.axis_size(TM)
    pairs = [(i, i + 1) for i in range(count - 1)]
    if not forward:
        pairs = [(j, i) for i, j in pairs]
    return lax.ppermute(value, TM, pairs)


def ring_shift(value, axis, shift):
    count = lax.axis_size(axis)
    return lax.ppermute(value, axis, [(i, (i + shift) % count) for i in range(count)])


def exchange(value, axis):
    return lax.all_to_all(value, axis, split_axis=0, concat_axis=0, tiled=True)


def route(first_tap, snip_count, unit_axis):
    count = first_tap[0].shape[0]
    col, row = first_tap
    mine, other = (col, row) if unit_axis == 0 else (row, col)
    reduce_axis = 1 - unit_axis
    block, block_other = mine // snip_count, other // snip_count
    crossing = mine % snip_count == snip_count - 1
    crossing_other = other % snip_count == snip_count - 1
    earlier = lax.broadcasted_iota(jnp.int32, (count, count), reduce_axis) < lax.broadcasted_iota(
        jnp.int32, (count, count), unit_axis
    )
    rank = jnp.sum(
        ((block == block_other) & crossing_other & earlier).astype(jnp.int32),
        axis=reduce_axis,
        keepdims=True,
    )
    target = block + (crossing & (rank % 2 == 1)).astype(jnp.int32)
    return target, mine - target * snip_count


def halved(value):
    high = lax.reduce_precision(value, 8, 7)
    rest = value - high
    middle = lax.reduce_precision(rest, 8, 7)
    return high, middle, rest - middle


def send_slots(bin_grad, tap_weight, tap_index, snip_count, peers):
    video_count, prop_count, bin_count, tap_count = tap_index.shape
    channels = bin_grad.shape[-1]
    units = video_count * prop_count * bin_count
    capacity = bin_count * ((video_count * prop_count + peers - 1) // peers)
    first = tap_index[..., 0].reshape(units)
    taps = (first[:, None], first[None, :])
    target_col, local = route(taps, snip_count, 0)
    target_row, _ = route(taps, snip_count, 1)
    earlier = lax.broadcasted_iota(jnp.int32, (units, units), 0) < lax.broadcasted_iota(
        jnp.int32, (units, units), 1
    )
    position = jnp.sum(
        ((target_col == target_row) & earlier).astype(jnp.int32), axis=0, keepdims=True
    )
    slot = target_row * capacity + position
    matches = (
        lax.broadcasted_iota(jnp.int32, (peers * capacity, units), 0) == slot
    ).astype(jnp.bfloat16)
    video = lax.broadcasted_iota(jnp.int32, (units, 1), 0) // (prop_count * bin_count)
    main = video_count * snip_count

    def line(step):
        at = local + step
        inside = video * snip_count + at
        edge = main + video + jnp.where(at < 0, 0, video_count)
        return jnp.where((at < 0) | (at >= snip_count), edge, inside)

    weights = tap_weight.reshape(units, tap_count)
    columns = []
    for step in range(2):
        where_to = line(step)
        columns += [(where_to // 256).astype(jnp.float32), (where_to % 256).astype(jnp.float32)]
        columns += list(halved(weights[:, step : step + 1]))
    lane = lax.broadcasted_iota(jnp.int32, (units, META), 1)
    meta = jnp.zeros((units, META), jnp.float32)
    for index, column in enumerate(columns):
        meta = jnp.where(lane == index, column, meta)
    payload = jnp.concatenate([bin_grad.reshape(units, channels), meta.astype(jnp.bfloat16)], axis=1)
    rows = jnp.dot(matches, payload, preferred_element_type=jnp.float32).astype(jnp.bfloat16)
    return rows.reshape(peers, capacity, channels + META)


def collect(got, channels, row_count):
    rows = got.reshape(-1, channels + META)
    grads = rows[:, :channels].astype(jnp.float32)
    meta = rows[:, channels:].astype(jnp.float32)
    meta_t = meta[:, :16].T
    total = jnp.zeros((row_count, channels), jnp.float32)
    for step in range(2):
        base = 5 * step
        where_to = (meta_t[base : base + 1] * 256.0 + meta_t[base + 1 : base + 2]).astype(jnp.int32)
        weight = meta[:, base + 2 : base + 3] + meta[:, base + 3 : base + 4] + meta[:, base + 4 : base + 5]
        tap_rows = (weight * grads).astype(jnp.bfloat16)
        table = (
            lax.broadcasted_iota(jnp.int32, (row_count, rows.shape[0]), 0) == where_to
        ).astype(jnp.bfloat16)
        total = total + jnp.dot(table, tap_rows, preferred_element_type=jnp.float32)
    return total


def finish_kernel(part_ref, low_in_ref, high_in_ref, after_ref, main_ref, before_ref, share_ref):
    videos, quarters = low_in_ref.shape[1], share_ref.shape[0]
    rows = main_ref.shape[0] // videos
    width = share_ref.shape[2]
    edges = part_ref.shape[0] - 2 * videos
    row = lax.broadcasted_iota(jnp.int32, (rows, part_ref.shape[1]), 0)
    lows, highs = [], []
    for video in range(videos):
        span = slice(video * rows, (video + 1) * rows)
        main = part_ref[span, :]
        main = main + jnp.where(row == 0, low_in_ref[1, video : video + 1, :], 0.0)
        main = main + jnp.where(row == rows - 1, high_in_ref[0, video : video + 1, :], 0.0)
        low = part_ref[edges + video : edges + video + 1, :] + low_in_ref[0, video : video + 1, :]
        high_at = edges + videos + video
        high = part_ref[high_at : high_at + 1, :] + high_in_ref[1, video : video + 1, :]
        before_ref[span, :] = jnp.where(row == 0, low, pltpu.roll(main, 1, 0)).astype(jnp.bfloat16)
        after_ref[span, :] = jnp.where(row == rows - 1, high, pltpu.roll(main, rows - 1, 0)).astype(
            jnp.bfloat16
        )
        main = main.astype(jnp.bfloat16)
        main_ref[span, :] = main
        for quarter in range(quarters):
            share_ref[quarter, span, :] = main[:, quarter * width : (quarter + 1) * width]
        lows.append(low)
        highs.append(high)
    pad = share_ref.shape[1] - edges - 2 * videos
    edge = jnp.concatenate(lows + highs + [jnp.zeros((pad, part_ref.shape[1]), jnp.float32)], axis=0)
    edge = edge.astype(jnp.bfloat16)
    for quarter in range(quarters):
        share_ref[quarter, edges:, :] = edge[:, quarter * width : (quarter + 1) * width]


def finish(partial, from_low, from_high, main_rows, quarters):
    channels = partial.shape[1]
    full = jax.ShapeDtypeStruct((main_rows, channels), jnp.bfloat16)
    share = jax.ShapeDtypeStruct((quarters, main_rows + 16, channels // quarters), jnp.bfloat16)
    return pl.pallas_call(
        finish_kernel,
        out_shape=(full, full, full, share),
        compiler_params=pltpu.CompilerParams(vmem_limit_bytes=40 * 2**20),
        cost_estimate=pl.CostEstimate(flops=0, bytes_accessed=8 * 2**20, transcendentals=0),
    )(partial, from_low, from_high)


def lags_kernel(videos, halo, grad_ref, out_ref):
    sources, block, width = grad_ref.shape
    rows = (block if not halo else block - 16) // videos
    main = rows * videos
    row = lax.broadcasted_iota(jnp.int32, (rows, width), 0)
    for source in range(sources):
        edge_low, edge_high = [], []
        if halo:
            edges = grad_ref[source, main:, :].astype(jnp.float32)
        for video in range(videos):
            span = slice(video * rows, (video + 1) * rows)
            grad = grad_ref[source, span, :].astype(jnp.float32)
            if halo:
                low, high = edges[video : video + 1], edges[videos + video : videos + video + 1]
            else:
                low, high = 0.0, 0.0
                edge_low.append(grad[:1])
                edge_high.append(grad[rows - 1 :])
            after = jnp.where(row == rows - 1, high, pltpu.roll(grad, rows - 1, 0))
            before = jnp.where(row == 0, low, pltpu.roll(grad, 1, 0))
            for index, part in enumerate((after, grad, before)):
                out_ref[source, span, index * width : (index + 1) * width] = part.astype(jnp.bfloat16)
        if not halo:
            zero = jnp.zeros((videos, width), jnp.float32)
            rest = jnp.zeros((out_ref.shape[1] - main - 2 * videos, width), jnp.float32)
            parts = (edge_low + [zero, rest], [zero, zero, rest], [zero] + edge_high + [rest])
            for index, part in enumerate(parts):
                out_ref[source, main:, index * width : (index + 1) * width] = jnp.concatenate(
                    part, axis=0
                ).astype(jnp.bfloat16)


def lags(gradient, videos, halo, lag_count):
    sources, block, width = gradient.shape
    rows = block - 16 if halo else block + 16
    return pl.pallas_call(
        lambda *refs: lags_kernel(videos, halo, *refs),
        out_shape=jax.ShapeDtypeStruct((sources, rows, lag_count * width), jnp.bfloat16),
        compiler_params=pltpu.CompilerParams(vmem_limit_bytes=40 * 2**20),
        cost_estimate=pl.CostEstimate(flops=0, bytes_accessed=4 * 2**20, transcendentals=0),
    )(gradient)


def filter_terms(inputs, lagged):
    inputs = inputs.reshape(-1, inputs.shape[-1])
    lagged = lagged.reshape(-1, lagged.shape[-1])
    return lax.dot_general(
        inputs, lagged, (((0,), (0,)), ((), ())), preferred_element_type=jnp.float32
    )


def reduce_core_x(terms):
    x_total, z_total, cores = (lax.axis_size(name) for name in TM)
    channels, outs = terms.shape
    each = channels // (x_total * z_total * cores)
    parts = terms.reshape(x_total * z_total, cores, each, outs)
    core = lax.axis_index("core")
    keep = lax.dynamic_index_in_dim(parts, core, 1, keepdims=False)
    give = lax.dynamic_index_in_dim(parts, 1 - core, 1, keepdims=False).astype(jnp.bfloat16)
    got = ring_shift(give, "core", 1)
    share = (keep + got.astype(jnp.float32)).astype(jnp.bfloat16)
    share = exchange(share.reshape(x_total, z_total * each, outs), "x")
    return jnp.sum(share.astype(jnp.float32), axis=0).reshape(z_total, each, outs)


def on_device(bin_grad, tap_weight, tap_index, features, preact, filter_second):
    video_count, snip_count, channels = features.shape
    peers = lax.axis_size(TM)
    quarters = lax.axis_size("video")
    lag_count = filter_second.shape[0]
    main_rows = video_count * snip_count
    sent = send_slots(bin_grad, tap_weight, tap_index, snip_count, peers)
    got = exchange(sent, TM)

    pre_values = preact.astype(jnp.float32).reshape(main_rows, channels)
    activation = jax.nn.silu(pre_values).astype(jnp.bfloat16)
    act_all = lax.all_gather(activation, "video", axis=0, tiled=False)
    after_send = sent[0, 0, 0] * 0
    edge_low = neighbours(features[:, -1] + after_send, True)
    edge_high = neighbours(features[:, 0] + after_send, False)
    spare = jnp.zeros((16 - 2 * video_count, channels), features.dtype)
    feature_rows = jnp.concatenate(
        [features.reshape(main_rows, channels), edge_low, edge_high, spare], axis=0
    )
    feature_all = lax.all_gather(feature_rows, "video", axis=0, tiled=False)

    partial = collect(got, channels, main_rows + 2 * video_count)
    ends = partial[:main_rows].reshape(video_count, snip_count, channels)
    low = partial[main_rows : main_rows + video_count]
    high = partial[main_rows + video_count :]
    from_low = neighbours(jnp.stack([ends[:, -1], high]), True)
    from_high = neighbours(jnp.stack([low, ends[:, 0]]), False)
    *windows, snippet_share = finish(partial, from_low, from_high, main_rows, quarters)
    snippet_share = exchange(snippet_share, "video")

    act_grad = jnp.zeros((main_rows, channels), jnp.float32)
    for window, taps in zip(windows, filter_second):
        act_grad = act_grad + lax.dot_general(
            window, taps, (((1,), (1,)), ((), ())), preferred_element_type=jnp.float32
        )
    pre_grad = (act_grad * silu_slope(pre_values)).astype(jnp.bfloat16)
    width = channels // quarters
    pre_share = jnp.stack([pre_grad[:, q * width : (q + 1) * width] for q in range(quarters)])
    pre_share = exchange(pre_share, "video")

    second = reduce_core_x(filter_terms(act_all, lags(snippet_share, video_count, True, lag_count)))
    first = reduce_core_x(filter_terms(feature_all, lags(pre_share, video_count, False, lag_count)))
    both = jnp.stack([first, second], axis=1).astype(jnp.bfloat16)
    mine = jnp.sum(exchange(both, "z").astype(jnp.float32), axis=0)

    place = lax.axis_index("video")
    held = [mine] + [ring_shift(mine, "video", shift) for shift in range(1, quarters)]
    blocks = []
    for quarter in range(quarters):
        block = held[0]
        for shift in range(1, quarters):
            block = jnp.where((place - shift) % quarters == quarter, held[shift], block)
        blocks.append(block.reshape(2, -1, lag_count, width))
    whole = jnp.concatenate(blocks, axis=-1)
    return (whole[0], whole[1])


def solution(mesh):
    shape = (mesh.shape["video"],) + TM_SIZES
    fine = Mesh(np.asarray(mesh.devices).reshape(shape), ("video",) + TM)
    return jax.shard_map(
        on_device,
        mesh=fine,
        in_specs=(
            P("video", TM, None, None),
            P("video", TM, None, None),
            P("video", TM, None, None),
            P("video", TM, None),
            P("video", TM, None),
            P(),
        ),
        out_specs=(P(TM, None, None), P(TM, None, None)),
        check_vma=False,
    )
```

```python
import jax
import jax.numpy as jnp
import numpy as np
from jax import lax
from jax.experimental import pallas as pl
from jax.experimental.pallas import tpu as pltpu
from jax.sharding import Mesh
from jax.sharding import PartitionSpec as P

TM = ("x", "z", "core")
TM_SIZES = (4, 8, 2)
META = 128


def silu_slope(values):
    sigma = jax.nn.sigmoid(values)
    return sigma * (1.0 + values * (1.0 - sigma))


def neighbours(value, forward):
    count = lax.axis_size(TM)
    pairs = [(i, i + 1) for i in range(count - 1)]
    if not forward:
        pairs = [(j, i) for i, j in pairs]
    return lax.ppermute(value, TM, pairs)


def ring_shift(value, axis, shift):
    count = lax.axis_size(axis)
    return lax.ppermute(value, axis, [(i, (i + shift) % count) for i in range(count)])


def exchange(value, axis):
    return lax.all_to_all(value, axis, split_axis=0, concat_axis=0, tiled=True)


def route(first_tap, snip_count, unit_axis):
    count = first_tap[0].shape[0]
    col, row = first_tap
    mine, other = (col, row) if unit_axis == 0 else (row, col)
    reduce_axis = 1 - unit_axis
    block, block_other = mine // snip_count, other // snip_count
    crossing = mine % snip_count == snip_count - 1
    crossing_other = other % snip_count == snip_count - 1
    earlier = lax.broadcasted_iota(jnp.int32, (count, count), reduce_axis) < lax.broadcasted_iota(
        jnp.int32, (count, count), unit_axis
    )
    rank = jnp.sum(
        ((block == block_other) & crossing_other & earlier).astype(jnp.int32),
        axis=reduce_axis,
        keepdims=True,
    )
    target = block + (crossing & (rank % 2 == 1)).astype(jnp.int32)
    return target, mine - target * snip_count


def halved(value):
    high = lax.reduce_precision(value, 8, 7)
    rest = value - high
    middle = lax.reduce_precision(rest, 8, 7)
    return high, middle, rest - middle


def send_slots(bin_grad, tap_weight, tap_index, snip_count, peers):
    video_count, prop_count, bin_count, tap_count = tap_index.shape
    channels = bin_grad.shape[-1]
    units = video_count * prop_count * bin_count
    capacity = bin_count * ((video_count * prop_count + peers - 1) // peers)
    first = tap_index[..., 0].reshape(units)
    taps = (first[:, None], first[None, :])
    target_col, local = route(taps, snip_count, 0)
    target_row, _ = route(taps, snip_count, 1)
    earlier = lax.broadcasted_iota(jnp.int32, (units, units), 0) < lax.broadcasted_iota(
        jnp.int32, (units, units), 1
    )
    position = jnp.sum(
        ((target_col == target_row) & earlier).astype(jnp.int32), axis=0, keepdims=True
    )
    slot = target_row * capacity + position
    matches = (
        lax.broadcasted_iota(jnp.int32, (peers * capacity, units), 0) == slot
    ).astype(jnp.bfloat16)
    video = lax.broadcasted_iota(jnp.int32, (units, 1), 0) // (prop_count * bin_count)
    main = video_count * snip_count

    def line(step):
        at = local + step
        inside = video * snip_count + at
        edge = main + video + jnp.where(at < 0, 0, video_count)
        return jnp.where((at < 0) | (at >= snip_count), edge, inside)

    weights = tap_weight.reshape(units, tap_count)
    columns = []
    for step in range(2):
        where_to = line(step)
        columns += [(where_to // 256).astype(jnp.float32), (where_to % 256).astype(jnp.float32)]
        columns += list(halved(weights[:, step : step + 1]))
    lane = lax.broadcasted_iota(jnp.int32, (units, META), 1)
    meta = jnp.zeros((units, META), jnp.float32)
    for index, column in enumerate(columns):
        meta = jnp.where(lane == index, column, meta)
    payload = jnp.concatenate([bin_grad.reshape(units, channels), meta.astype(jnp.bfloat16)], axis=1)
    rows = jnp.dot(matches, payload, preferred_element_type=jnp.float32).astype(jnp.bfloat16)
    return rows.reshape(peers, capacity, channels + META)


def collect(got, channels, row_count):
    rows = got.reshape(-1, channels + META)
    grads = rows[:, :channels].astype(jnp.float32)
    meta = rows[:, channels:].astype(jnp.float32)
    meta_t = meta[:, :16].T
    total = jnp.zeros((row_count, channels), jnp.float32)
    for step in range(2):
        base = 5 * step
        where_to = (meta_t[base : base + 1] * 256.0 + meta_t[base + 1 : base + 2]).astype(jnp.int32)
        weight = meta[:, base + 2 : base + 3] + meta[:, base + 3 : base + 4] + meta[:, base + 4 : base + 5]
        tap_rows = (weight * grads).astype(jnp.bfloat16)
        table = (
            lax.broadcasted_iota(jnp.int32, (row_count, rows.shape[0]), 0) == where_to
        ).astype(jnp.bfloat16)
        total = total + jnp.dot(table, tap_rows, preferred_element_type=jnp.float32)
    return total


def finish_kernel(part_ref, low_in_ref, high_in_ref, after_ref, main_ref, before_ref, share_ref):
    videos, quarters = low_in_ref.shape[1], share_ref.shape[0]
    width = share_ref.shape[2]
    edges = part_ref.shape[0] - 2 * videos
    rows = edges // videos
    row = lax.broadcasted_iota(jnp.int32, (rows, part_ref.shape[1]), 0)
    low_edges, high_edges = ([], [], []), ([], [], [])
    for video in range(videos):
        span = slice(video * rows, (video + 1) * rows)
        main = part_ref[span, :]
        main = main + jnp.where(row == 0, low_in_ref[2, video : video + 1, :], 0.0)
        main = main + jnp.where(row == rows - 1, high_in_ref[0, video : video + 1, :], 0.0)
        low = part_ref[edges + video : edges + video + 1, :] + low_in_ref[1, video : video + 1, :]
        high_at = edges + videos + video
        high = part_ref[high_at : high_at + 1, :] + high_in_ref[1, video : video + 1, :]
        before_ref[span, :] = jnp.where(row == 0, low, pltpu.roll(main, 1, 0)).astype(jnp.bfloat16)
        after_ref[span, :] = jnp.where(row == rows - 1, high, pltpu.roll(main, rows - 1, 0)).astype(
            jnp.bfloat16
        )
        for index, part in enumerate((main[:1], low, low_in_ref[0, video : video + 1, :])):
            low_edges[index].append(part)
        for index, part in enumerate((high_in_ref[2, video : video + 1, :], high, main[rows - 1 :])):
            high_edges[index].append(part)
        main = main.astype(jnp.bfloat16)
        main_ref[span, :] = main
        for quarter in range(quarters):
            share_ref[quarter, span, :] = main[:, quarter * width : (quarter + 1) * width]
    spare = [jnp.zeros((main_ref.shape[0] - edges - 2 * videos, part_ref.shape[1]), jnp.float32)]
    for index, ref in enumerate((after_ref, main_ref, before_ref)):
        edge = jnp.concatenate(low_edges[index] + high_edges[index] + spare, axis=0)
        edge = edge.astype(jnp.bfloat16)
        ref[edges:, :] = edge
        if ref is main_ref:
            for quarter in range(quarters):
                share_ref[quarter, edges:, :] = edge[:, quarter * width : (quarter + 1) * width]


def finish(partial, from_low, from_high, main_rows, quarters):
    channels = partial.shape[1]
    full = jax.ShapeDtypeStruct((main_rows + 16, channels), jnp.bfloat16)
    share = jax.ShapeDtypeStruct((quarters, main_rows + 16, channels // quarters), jnp.bfloat16)
    return pl.pallas_call(
        finish_kernel,
        out_shape=(full, full, full, share),
        compiler_params=pltpu.CompilerParams(vmem_limit_bytes=40 * 2**20),
        cost_estimate=pl.CostEstimate(flops=0, bytes_accessed=8 * 2**20, transcendentals=0),
    )(partial, from_low, from_high)


def terms_kernel(videos, source_count, order_ref, grad_ref, *refs):
    input_refs, (keep_ref, give_ref, lag_ref) = refs[:-3], refs[-3:]
    width = grad_ref.shape[2]
    main = grad_ref.shape[1] - 16
    rows = main // videos
    groups, each, outs = keep_ref.shape
    core = order_ref[source_count]
    row = lax.broadcasted_iota(jnp.int32, (rows, width), 0)
    for source in range(source_count):
        at = order_ref[source]
        edges = grad_ref[at, main:, :].astype(jnp.float32)
        for video in range(videos):
            span = slice(video * rows, (video + 1) * rows)
            grad = grad_ref[at, span, :].astype(jnp.float32)
            low, high = edges[video : video + 1], edges[videos + video : videos + video + 1]
            after = jnp.where(row == rows - 1, high, pltpu.roll(grad, rows - 1, 0))
            before = jnp.where(row == 0, low, pltpu.roll(grad, 1, 0))
            for index, part in enumerate((after, grad, before)):
                lag_ref[
                    source * main + video * rows : source * main + (video + 1) * rows,
                    index * width : (index + 1) * width,
                ] = part.astype(jnp.bfloat16)
    channels = groups * 2 * each
    step = min(256, channels)
    for start in range(0, channels, step):
        total = jnp.zeros((step, outs), jnp.float32)
        for source in range(source_count):
            if len(input_refs) == 1:
                block = input_refs[0][source, :, start : start + step]
            else:
                block = input_refs[source][:, start : start + step]
            total = total + lax.dot_general(
                block,
                lag_ref[source * main : (source + 1) * main, :],
                (((0,), (0,)), ((), ())),
                preferred_element_type=jnp.float32,
            )
        total = total.reshape(step // (2 * each), 2, each, outs)
        first, second = total[:, 0], total[:, 1]
        span = slice(start // (2 * each), (start + step) // (2 * each))
        keep_ref[span] = jnp.where(core == 0, first, second)
        give_ref[span] = jnp.where(core == 0, second, first).astype(jnp.bfloat16)


def filter_terms(inputs, gradient, order, videos, lag_count, each):
    source_count, block, width = gradient.shape
    channels = inputs[0].shape[-1]
    shape = (channels // (2 * each), each, lag_count * width)
    rows = source_count * (block - 16)
    vmem = pl.BlockSpec(memory_space=pltpu.VMEM)
    return pl.pallas_call(
        lambda *refs: terms_kernel(videos, source_count, *refs),
        out_shape=(
            jax.ShapeDtypeStruct(shape, jnp.float32),
            jax.ShapeDtypeStruct(shape, jnp.bfloat16),
        ),
        in_specs=[pl.BlockSpec(memory_space=pltpu.SMEM)] + [vmem] * (1 + len(inputs)),
        out_specs=(vmem, vmem),
        scratch_shapes=[pltpu.VMEM((rows, lag_count * width), jnp.bfloat16)],
        compiler_params=pltpu.CompilerParams(vmem_limit_bytes=40 * 2**20),
        cost_estimate=pl.CostEstimate(
            flops=2 * rows * channels * lag_count * width,
            bytes_accessed=10 * 2**20,
            transcendentals=0,
        ),
    )(order, gradient, *inputs)


def reduce_core_x(keep, give):
    x_total, z_total = lax.axis_size("x"), lax.axis_size("z")
    groups, each, outs = keep.shape
    got = ring_shift(give, "core", 1)
    share = (keep + got.astype(jnp.float32)).astype(jnp.bfloat16)
    share = exchange(share.reshape(x_total, z_total * each, outs), "x")
    return jnp.sum(share.astype(jnp.float32), axis=0).reshape(z_total, each, outs)


def on_device(bin_grad, tap_weight, tap_index, features, preact, filter_second):
    video_count, snip_count, channels = features.shape
    peers = lax.axis_size(TM)
    quarters = lax.axis_size("video")
    place, core = lax.axis_index("video"), lax.axis_index("core")
    lag_count = filter_second.shape[0]
    main_rows = video_count * snip_count
    each = channels // peers
    sent = send_slots(bin_grad, tap_weight, tap_index, snip_count, peers)
    got = exchange(sent, TM)

    pre_values = preact.astype(jnp.float32).reshape(main_rows, channels)
    activation = jax.nn.silu(pre_values).astype(jnp.bfloat16)
    act_all = lax.all_gather(activation, "video", axis=0, tiled=False)
    after_send = sent[0, 0, 0] * 0
    feature_rows = features.reshape(main_rows, channels) + after_send
    feature_all = [feature_rows] + [
        ring_shift(feature_rows, "video", shift) for shift in range(1, quarters)
    ]
    pre_low = neighbours(preact[:, -1] + after_send, True)
    pre_high = neighbours(preact[:, 0] + after_send, False)
    at = lax.axis_index(TM)
    edge_slope = jnp.concatenate(
        [
            jnp.where(at > 0, silu_slope(pre_low.astype(jnp.float32)), 0.0),
            jnp.where(at < peers - 1, silu_slope(pre_high.astype(jnp.float32)), 0.0),
            jnp.zeros((16 - 2 * video_count, channels), jnp.float32),
        ],
        axis=0,
    )

    partial = collect(got, channels, main_rows + 2 * video_count)
    ends = partial[:main_rows].reshape(video_count, snip_count, channels)
    low = partial[main_rows : main_rows + video_count]
    high = partial[main_rows + video_count :]
    from_low = neighbours(jnp.stack([ends[:, -2], ends[:, -1], high]), True)
    from_high = neighbours(jnp.stack([low, ends[:, 0], ends[:, 1]]), False)
    *windows, snippet_share = finish(partial, from_low, from_high, main_rows, quarters)
    snippet_share = exchange(snippet_share, "video")

    act_grad = jnp.zeros((main_rows + 16, channels), jnp.float32)
    for window, taps in zip(windows, filter_second):
        act_grad = act_grad + lax.dot_general(
            window, taps, (((1,), (1,)), ((), ())), preferred_element_type=jnp.float32
        )
    slope = jnp.concatenate([silu_slope(pre_values), edge_slope], axis=0)
    pre_grad = (act_grad * slope).astype(jnp.bfloat16)
    pre_grad = pre_grad + snippet_share[0, 0, 0] * 0
    width = channels // quarters
    pre_share = jnp.stack([pre_grad[:, q * width : (q + 1) * width] for q in range(quarters)])
    pre_share = exchange(pre_share, "video")

    in_order = [jnp.int32(source) for source in range(quarters)]
    around = [(place + quarters - source) % quarters for source in range(quarters)]
    second = filter_terms(
        [act_all], snippet_share, jnp.stack(in_order + [core]), video_count, lag_count, each
    )
    first = filter_terms(
        feature_all, pre_share, jnp.stack(around + [core]), video_count, lag_count, each
    )
    second, first = reduce_core_x(*second), reduce_core_x(*first)
    both = jnp.stack([first, second], axis=1).astype(jnp.bfloat16)
    mine = jnp.sum(exchange(both, "z").astype(jnp.float32), axis=0)

    held = [mine] + [ring_shift(mine, "video", shift) for shift in range(1, quarters)]
    blocks = []
    for quarter in range(quarters):
        block = held[0]
        for shift in range(1, quarters):
            block = jnp.where((place - shift) % quarters == quarter, held[shift], block)
        blocks.append(block.reshape(2, -1, lag_count, width))
    whole = jnp.concatenate(blocks, axis=-1)
    return (whole[0], whole[1])


def solution(mesh):
    shape = (mesh.shape["video"],) + TM_SIZES
    fine = Mesh(np.asarray(mesh.devices).reshape(shape), ("video",) + TM)
    return jax.shard_map(
        on_device,
        mesh=fine,
        in_specs=(
            P("video", TM, None, None),
            P("video", TM, None, None),
            P("video", TM, None, None),
            P("video", TM, None),
            P("video", TM, None),
            P(),
        ),
        out_specs=(P(TM, None, None), P(TM, None, None)),
        check_vma=False,
    )
```

```python
import jax
import jax.numpy as jnp
import numpy as np
from jax import lax
from jax.experimental import pallas as pl
from jax.experimental.pallas import tpu as pltpu
from jax.sharding import Mesh
from jax.sharding import PartitionSpec as P

TM = ("x", "z", "core")
TM_SIZES = (4, 8, 2)
META = 128


def silu_slope(values):
    sigma = jax.nn.sigmoid(values)
    return sigma * (1.0 + values * (1.0 - sigma))


def neighbours(value, forward):
    count = lax.axis_size(TM)
    pairs = [(i, i + 1) for i in range(count - 1)]
    if not forward:
        pairs = [(j, i) for i, j in pairs]
    return lax.ppermute(value, TM, pairs)


def ring_shift(value, axis, shift):
    count = lax.axis_size(axis)
    return lax.ppermute(value, axis, [(i, (i + shift) % count) for i in range(count)])


def around_video(rows):
    count = lax.axis_size("video")
    if count != 4:
        return [[rows]] + [[ring_shift(rows, "video", shift)] for shift in range(1, count)]
    half = rows.shape[0] // 2
    below, above = ring_shift(rows, "video", 1), ring_shift(rows, "video", 3)
    far = [ring_shift(below[:half], "video", 1), ring_shift(above[half:], "video", 3)]
    return [[rows], [below], far, [above]]


def exchange(value, axis):
    return lax.all_to_all(value, axis, split_axis=0, concat_axis=0, tiled=True)


def route(first_tap, snip_count, unit_axis):
    count = first_tap[0].shape[0]
    col, row = first_tap
    mine, other = (col, row) if unit_axis == 0 else (row, col)
    reduce_axis = 1 - unit_axis
    block, block_other = mine // snip_count, other // snip_count
    crossing = mine % snip_count == snip_count - 1
    crossing_other = other % snip_count == snip_count - 1
    earlier = lax.broadcasted_iota(jnp.int32, (count, count), reduce_axis) < lax.broadcasted_iota(
        jnp.int32, (count, count), unit_axis
    )
    rank = jnp.sum(
        ((block == block_other) & crossing_other & earlier).astype(jnp.int32),
        axis=reduce_axis,
        keepdims=True,
    )
    target = block + (crossing & (rank % 2 == 1)).astype(jnp.int32)
    return target, mine - target * snip_count


def halved(value):
    high = lax.reduce_precision(value, 8, 7)
    rest = value - high
    middle = lax.reduce_precision(rest, 8, 7)
    return high, middle, rest - middle


def send_slots(bin_grad, tap_weight, tap_index, snip_count, peers):
    video_count, prop_count, bin_count, tap_count = tap_index.shape
    channels = bin_grad.shape[-1]
    units = video_count * prop_count * bin_count
    capacity = bin_count * ((video_count * prop_count + peers - 1) // peers)
    first = tap_index[..., 0].reshape(units)
    taps = (first[:, None], first[None, :])
    target_col, local = route(taps, snip_count, 0)
    target_row, _ = route(taps, snip_count, 1)
    earlier = lax.broadcasted_iota(jnp.int32, (units, units), 0) < lax.broadcasted_iota(
        jnp.int32, (units, units), 1
    )
    position = jnp.sum(
        ((target_col == target_row) & earlier).astype(jnp.int32), axis=0, keepdims=True
    )
    slot = target_row * capacity + position
    matches = (
        lax.broadcasted_iota(jnp.int32, (peers * capacity, units), 0) == slot
    ).astype(jnp.bfloat16)
    video = lax.broadcasted_iota(jnp.int32, (units, 1), 0) // (prop_count * bin_count)
    main = video_count * snip_count

    def line(step):
        at = local + step
        inside = video * snip_count + at
        edge = main + video + jnp.where(at < 0, 0, video_count)
        return jnp.where((at < 0) | (at >= snip_count), edge, inside)

    weights = tap_weight.reshape(units, tap_count)
    columns = []
    for step in range(2):
        where_to = line(step)
        columns += [(where_to // 256).astype(jnp.float32), (where_to % 256).astype(jnp.float32)]
        columns += list(halved(weights[:, step : step + 1]))
    lane = lax.broadcasted_iota(jnp.int32, (units, META), 1)
    meta = jnp.zeros((units, META), jnp.float32)
    for index, column in enumerate(columns):
        meta = jnp.where(lane == index, column, meta)
    payload = jnp.concatenate([bin_grad.reshape(units, channels), meta.astype(jnp.bfloat16)], axis=1)
    rows = jnp.dot(matches, payload, preferred_element_type=jnp.float32).astype(jnp.bfloat16)
    return rows.reshape(peers, capacity, channels + META)


def collect(got, channels, row_count):
    rows = got.reshape(-1, channels + META)
    grads = rows[:, :channels].astype(jnp.float32)
    meta = rows[:, channels:].astype(jnp.float32)
    meta_t = meta[:, :16].T
    total = jnp.zeros((row_count, channels), jnp.float32)
    for step in range(2):
        base = 5 * step
        where_to = (meta_t[base : base + 1] * 256.0 + meta_t[base + 1 : base + 2]).astype(jnp.int32)
        weight = meta[:, base + 2 : base + 3] + meta[:, base + 3 : base + 4] + meta[:, base + 4 : base + 5]
        tap_rows = (weight * grads).astype(jnp.bfloat16)
        table = (
            lax.broadcasted_iota(jnp.int32, (row_count, rows.shape[0]), 0) == where_to
        ).astype(jnp.bfloat16)
        total = total + jnp.dot(table, tap_rows, preferred_element_type=jnp.float32)
    return total


def finish_kernel(part_ref, low_in_ref, high_in_ref, after_ref, main_ref, before_ref, share_ref):
    videos, quarters = low_in_ref.shape[1], share_ref.shape[0]
    width = share_ref.shape[2]
    edges = part_ref.shape[0] - 2 * videos
    rows = edges // videos
    row = lax.broadcasted_iota(jnp.int32, (rows, part_ref.shape[1]), 0)
    low_edges, high_edges = ([], [], []), ([], [], [])
    for video in range(videos):
        span = slice(video * rows, (video + 1) * rows)
        main = part_ref[span, :]
        main = main + jnp.where(row == 0, low_in_ref[2, video : video + 1, :], 0.0)
        main = main + jnp.where(row == rows - 1, high_in_ref[0, video : video + 1, :], 0.0)
        low = part_ref[edges + video : edges + video + 1, :] + low_in_ref[1, video : video + 1, :]
        high_at = edges + videos + video
        high = part_ref[high_at : high_at + 1, :] + high_in_ref[1, video : video + 1, :]
        before_ref[span, :] = jnp.where(row == 0, low, pltpu.roll(main, 1, 0)).astype(jnp.bfloat16)
        after_ref[span, :] = jnp.where(row == rows - 1, high, pltpu.roll(main, rows - 1, 0)).astype(
            jnp.bfloat16
        )
        for index, part in enumerate((main[:1], low, low_in_ref[0, video : video + 1, :])):
            low_edges[index].append(part)
        for index, part in enumerate((high_in_ref[2, video : video + 1, :], high, main[rows - 1 :])):
            high_edges[index].append(part)
        main = main.astype(jnp.bfloat16)
        main_ref[span, :] = main
        for quarter in range(quarters):
            share_ref[quarter, span, :] = main[:, quarter * width : (quarter + 1) * width]
    spare = [jnp.zeros((main_ref.shape[0] - edges - 2 * videos, part_ref.shape[1]), jnp.float32)]
    for index, ref in enumerate((after_ref, main_ref, before_ref)):
        edge = jnp.concatenate(low_edges[index] + high_edges[index] + spare, axis=0)
        edge = edge.astype(jnp.bfloat16)
        ref[edges:, :] = edge
        if ref is main_ref:
            for quarter in range(quarters):
                share_ref[quarter, edges:, :] = edge[:, quarter * width : (quarter + 1) * width]


def finish(partial, from_low, from_high, main_rows, quarters):
    channels = partial.shape[1]
    full = jax.ShapeDtypeStruct((main_rows + 16, channels), jnp.bfloat16)
    share = jax.ShapeDtypeStruct((quarters, main_rows + 16, channels // quarters), jnp.bfloat16)
    return pl.pallas_call(
        finish_kernel,
        out_shape=(full, full, full, share),
        compiler_params=pltpu.CompilerParams(vmem_limit_bytes=14 * 2**20),
        cost_estimate=pl.CostEstimate(flops=0, bytes_accessed=8 * 2**20, transcendentals=0),
    )(partial, from_low, from_high)


def pre_grad_kernel(after_ref, main_ref, before_ref, taps_ref, pre_ref, edge_ref, out_ref):
    total = jnp.zeros(out_ref.shape[1:], jnp.float32)
    for index, ref in enumerate((after_ref, main_ref, before_ref)):
        total = total + lax.dot_general(
            ref[...], taps_ref[index], (((1,), (1,)), ((), ())), preferred_element_type=jnp.float32
        )
    slope = jnp.concatenate([silu_slope(pre_ref[...].astype(jnp.float32)), edge_ref[...]], axis=0)
    out_ref[0] = (total * slope).astype(jnp.bfloat16)


def pre_grad_share(windows, filter_second, pre_rows, edge_slope, quarters):
    lag_count, channels, _ = filter_second.shape
    rows, width = windows[0].shape[0], channels // quarters
    whole = pl.BlockSpec((rows, channels), lambda q: (0, 0))
    return pl.pallas_call(
        pre_grad_kernel,
        grid=(quarters,),
        out_shape=jax.ShapeDtypeStruct((quarters, rows, width), jnp.bfloat16),
        in_specs=[whole] * 3
        + [
            pl.BlockSpec((lag_count, width, channels), lambda q: (0, q, 0)),
            pl.BlockSpec((pre_rows.shape[0], width), lambda q: (0, q)),
            pl.BlockSpec((16, width), lambda q: (0, q)),
        ],
        out_specs=pl.BlockSpec((1, rows, width), lambda q: (q, 0, 0)),
        compiler_params=pltpu.CompilerParams(vmem_limit_bytes=20 * 2**20),
        cost_estimate=pl.CostEstimate(
            flops=2 * rows * channels * channels * lag_count,
            bytes_accessed=11 * 2**20,
            transcendentals=rows * channels,
        ),
    )(*windows, filter_second, pre_rows, edge_slope)


def terms_kernel(videos, source_count, pieces, order_ref, grad_ref, *refs):
    input_refs, (keep_ref, give_ref, lag_ref) = refs[:-3], refs[-3:]
    width = grad_ref.shape[2]
    main = grad_ref.shape[1] - 16
    rows = main // videos
    groups, each, outs = keep_ref.shape
    core = order_ref[source_count]
    row = lax.broadcasted_iota(jnp.int32, (rows, width), 0)
    for source in range(source_count):
        at = order_ref[source]
        edges = grad_ref[at, main:, :].astype(jnp.float32)
        for video in range(videos):
            span = slice(video * rows, (video + 1) * rows)
            grad = grad_ref[at, span, :].astype(jnp.float32)
            low, high = edges[video : video + 1], edges[videos + video : videos + video + 1]
            after = jnp.where(row == rows - 1, high, pltpu.roll(grad, rows - 1, 0))
            before = jnp.where(row == 0, low, pltpu.roll(grad, 1, 0))
            for index, part in enumerate((after, grad, before)):
                lag_ref[
                    source * main + video * rows : source * main + (video + 1) * rows,
                    index * width : (index + 1) * width,
                ] = part.astype(jnp.bfloat16)
    channels = groups * 2 * each
    step = min(256, channels)
    for start in range(0, channels, step):
        total = jnp.zeros((step, outs), jnp.float32)
        for ref, (offset, count) in zip(input_refs, pieces):
            total = total + lax.dot_general(
                ref[:, start : start + step],
                lag_ref[offset : offset + count, :],
                (((0,), (0,)), ((), ())),
                preferred_element_type=jnp.float32,
            )
        total = total.reshape(step // (2 * each), 2, each, outs)
        first, second = total[:, 0], total[:, 1]
        span = slice(start // (2 * each), (start + step) // (2 * each))
        keep_ref[span] = jnp.where(core == 0, first, second)
        give_ref[span] = jnp.where(core == 0, second, first).astype(jnp.bfloat16)


def filter_terms(inputs, gradient, order, videos, lag_count, each):
    source_count, block, width = gradient.shape
    channels = inputs[0].shape[-1]
    pieces, offset = [], 0
    for piece in inputs:
        pieces.append((offset, piece.shape[0]))
        offset += piece.shape[0]
    shape = (channels // (2 * each), each, lag_count * width)
    rows = source_count * (block - 16)
    vmem = pl.BlockSpec(memory_space=pltpu.VMEM)
    return pl.pallas_call(
        lambda *refs: terms_kernel(videos, source_count, pieces, *refs),
        out_shape=(
            jax.ShapeDtypeStruct(shape, jnp.float32),
            jax.ShapeDtypeStruct(shape, jnp.bfloat16),
        ),
        in_specs=[pl.BlockSpec(memory_space=pltpu.SMEM)] + [vmem] * (1 + len(inputs)),
        out_specs=(vmem, vmem),
        scratch_shapes=[pltpu.VMEM((rows, lag_count * width), jnp.bfloat16)],
        compiler_params=pltpu.CompilerParams(vmem_limit_bytes=20 * 2**20),
        cost_estimate=pl.CostEstimate(
            flops=2 * rows * channels * lag_count * width,
            bytes_accessed=10 * 2**20,
            transcendentals=0,
        ),
    )(order, gradient, *inputs)


def share_by_core(keep, give):
    got = ring_shift(give, "core", 1)
    return (keep + got.astype(jnp.float32)).astype(jnp.bfloat16)


def sum_over_x(share):
    x_total, z_total = lax.axis_size("x"), lax.axis_size("z")
    groups, each, outs = share.shape
    share = exchange(share.reshape(x_total, z_total * each, outs), "x")
    return jnp.sum(share.astype(jnp.float32), axis=0).reshape(z_total, each, outs)


def on_device(bin_grad, tap_weight, tap_index, features, preact, filter_second):
    video_count, snip_count, channels = features.shape
    peers = lax.axis_size(TM)
    quarters = lax.axis_size("video")
    place, core = lax.axis_index("video"), lax.axis_index("core")
    lag_count = filter_second.shape[0]
    main_rows = video_count * snip_count
    each = channels // peers
    sent = send_slots(bin_grad, tap_weight, tap_index, snip_count, peers)
    got = exchange(sent, TM)

    pre_values = preact.astype(jnp.float32).reshape(main_rows, channels)
    activation = jax.nn.silu(pre_values).astype(jnp.bfloat16)
    feature_all = lax.all_gather(
        features.reshape(main_rows, channels), "video", axis=0, tiled=False
    )
    act_all = around_video(activation + sent[0, 0, 0] * 0)

    partial = collect(got, channels, main_rows + 2 * video_count)
    ends = partial[:main_rows].reshape(video_count, snip_count, channels)
    low = partial[main_rows : main_rows + video_count]
    high = partial[main_rows + video_count :]
    pre_ends = pre_values.reshape(ends.shape)
    from_low = neighbours(jnp.stack([ends[:, -2], ends[:, -1], high, pre_ends[:, -1]]), True)
    from_high = neighbours(jnp.stack([low, ends[:, 0], ends[:, 1], pre_ends[:, 0]]), False)
    *windows, snippet_share = finish(partial, from_low, from_high, main_rows, quarters)
    snippet_share = exchange(snippet_share, "video")

    at = lax.axis_index(TM)
    edge_slope = jnp.concatenate(
        [
            jnp.where(at > 0, silu_slope(from_low[3]), 0.0),
            jnp.where(at < peers - 1, silu_slope(from_high[3]), 0.0),
            jnp.zeros((16 - 2 * video_count, channels), jnp.float32),
        ],
        axis=0,
    )
    pre_rows = preact.reshape(main_rows, channels)
    pre_share = pre_grad_share(windows, filter_second, pre_rows, edge_slope, quarters)
    after_pre = (pre_share[0, 0, 0] * 0).astype(jnp.int32)
    pre_share = exchange(pre_share + snippet_share[0, 0, 0] * 0, "video")
    width = channels // quarters

    in_order = [jnp.int32(source) for source in range(quarters)]
    around = [(place + quarters - source) % quarters for source in range(quarters)]
    act_pieces = [piece for source in act_all for piece in source]
    second = share_by_core(
        *filter_terms(
            act_pieces,
            snippet_share,
            jnp.stack(around + [core]) + after_pre,
            video_count,
            lag_count,
            each,
        )
    )
    turn = jnp.stack(in_order + [core]) + (second[0, 0, 0] * 0).astype(jnp.int32)
    feature_all = feature_all.reshape(-1, channels)
    first = share_by_core(
        *filter_terms([feature_all], pre_share, turn, video_count, lag_count, each)
    )
    second, first = sum_over_x(second), sum_over_x(first)
    both = jnp.stack([first, second], axis=1).astype(jnp.bfloat16)
    mine = jnp.sum(exchange(both, "z").astype(jnp.float32), axis=0)

    held = [mine] + [ring_shift(mine, "video", shift) for shift in range(1, quarters)]
    blocks = []
    for quarter in range(quarters):
        block = held[0]
        for shift in range(1, quarters):
            block = jnp.where((place - shift) % quarters == quarter, held[shift], block)
        blocks.append(block.reshape(2, -1, lag_count, width))
    whole = jnp.concatenate(blocks, axis=-1)
    return (whole[0], whole[1])


def solution(mesh):
    shape = (mesh.shape["video"],) + TM_SIZES
    fine = Mesh(np.asarray(mesh.devices).reshape(shape), ("video",) + TM)
    return jax.shard_map(
        on_device,
        mesh=fine,
        in_specs=(
            P("video", TM, None, None),
            P("video", TM, None, None),
            P("video", TM, None, None),
            P("video", TM, None),
            P("video", TM, None),
            P(),
        ),
        out_specs=(P(TM, None, None), P(TM, None, None)),
        check_vma=False,
    )
```

```python
import jax
import jax.numpy as jnp
import numpy as np
from jax import lax
from jax.experimental import pallas as pl
from jax.experimental.pallas import tpu as pltpu
from jax.sharding import Mesh
from jax.sharding import PartitionSpec as P

TM = ("x", "z", "core")
TM_SIZES = (4, 8, 2)
META = 128


def silu_slope(values):
    sigma = jax.nn.sigmoid(values)
    return sigma * (1.0 + values * (1.0 - sigma))


def neighbours(value, forward):
    count = lax.axis_size(TM)
    pairs = [(i, i + 1) for i in range(count - 1)]
    if not forward:
        pairs = [(j, i) for i, j in pairs]
    return lax.ppermute(value, TM, pairs)


def ring_shift(value, axis, shift):
    count = lax.axis_size(axis)
    return lax.ppermute(value, axis, [(i, (i + shift) % count) for i in range(count)])


def exchange(value, axis):
    return lax.all_to_all(value, axis, split_axis=0, concat_axis=0, tiled=True)


def route(first_tap, snip_count, unit_axis):
    count = first_tap[0].shape[0]
    col, row = first_tap
    mine, other = (col, row) if unit_axis == 0 else (row, col)
    reduce_axis = 1 - unit_axis
    block, block_other = mine // snip_count, other // snip_count
    crossing = mine % snip_count == snip_count - 1
    crossing_other = other % snip_count == snip_count - 1
    earlier = lax.broadcasted_iota(jnp.int32, (count, count), reduce_axis) < lax.broadcasted_iota(
        jnp.int32, (count, count), unit_axis
    )
    rank = jnp.sum(
        ((block == block_other) & crossing_other & earlier).astype(jnp.int32),
        axis=reduce_axis,
        keepdims=True,
    )
    target = block + (crossing & (rank % 2 == 1)).astype(jnp.int32)
    return target, mine - target * snip_count


def halved(value):
    high = lax.reduce_precision(value, 8, 7)
    rest = value - high
    middle = lax.reduce_precision(rest, 8, 7)
    return high, middle, rest - middle


def send_slots(bin_grad, tap_weight, tap_index, snip_count, peers):
    video_count, prop_count, bin_count, tap_count = tap_index.shape
    channels = bin_grad.shape[-1]
    units = video_count * prop_count * bin_count
    capacity = bin_count * ((video_count * prop_count + peers - 1) // peers)
    first = tap_index[..., 0].reshape(units)
    taps = (first[:, None], first[None, :])
    target_col, local = route(taps, snip_count, 0)
    target_row, _ = route(taps, snip_count, 1)
    earlier = lax.broadcasted_iota(jnp.int32, (units, units), 0) < lax.broadcasted_iota(
        jnp.int32, (units, units), 1
    )
    position = jnp.sum(
        ((target_col == target_row) & earlier).astype(jnp.int32), axis=0, keepdims=True
    )
    slot = target_row * capacity + position
    matches = (
        lax.broadcasted_iota(jnp.int32, (peers * capacity, units), 0) == slot
    ).astype(jnp.bfloat16)
    video = lax.broadcasted_iota(jnp.int32, (units, 1), 0) // (prop_count * bin_count)
    main = video_count * snip_count

    def line(step):
        at = local + step
        inside = video * snip_count + at
        edge = main + video + jnp.where(at < 0, 0, video_count)
        return jnp.where((at < 0) | (at >= snip_count), edge, inside)

    weights = tap_weight.reshape(units, tap_count)
    columns = []
    for step in range(2):
        where_to = line(step)
        columns += [(where_to // 256).astype(jnp.float32), (where_to % 256).astype(jnp.float32)]
        columns += list(halved(weights[:, step : step + 1]))
    lane = lax.broadcasted_iota(jnp.int32, (units, META), 1)
    meta = jnp.zeros((units, META), jnp.float32)
    for index, column in enumerate(columns):
        meta = jnp.where(lane == index, column, meta)
    payload = jnp.concatenate([bin_grad.reshape(units, channels), meta.astype(jnp.bfloat16)], axis=1)
    rows = jnp.dot(matches, payload, preferred_element_type=jnp.float32).astype(jnp.bfloat16)
    return rows.reshape(peers, capacity, channels + META)


def collect(got, channels, row_count):
    rows = got.reshape(-1, channels + META)
    grads = rows[:, :channels].astype(jnp.float32)
    meta = rows[:, channels:].astype(jnp.float32)
    meta_t = meta[:, :16].T
    total = jnp.zeros((row_count, channels), jnp.float32)
    for step in range(2):
        base = 5 * step
        where_to = (meta_t[base : base + 1] * 256.0 + meta_t[base + 1 : base + 2]).astype(jnp.int32)
        weight = meta[:, base + 2 : base + 3] + meta[:, base + 3 : base + 4] + meta[:, base + 4 : base + 5]
        tap_rows = (weight * grads).astype(jnp.bfloat16)
        table = (
            lax.broadcasted_iota(jnp.int32, (row_count, rows.shape[0]), 0) == where_to
        ).astype(jnp.bfloat16)
        total = total + jnp.dot(table, tap_rows, preferred_element_type=jnp.float32)
    return total


def grads_kernel(
    valid_ref,
    part_ref,
    low_in_ref,
    high_in_ref,
    taps_ref,
    pre_ref,
    pre_low_ref,
    pre_high_ref,
    share_ref,
    pre_share_ref,
    windows_ref,
):
    videos = low_in_ref.shape[1]
    width = share_ref.shape[2]
    edges = part_ref.shape[0] - 2 * videos
    rows = edges // videos
    channels = part_ref.shape[1]
    quarter = pl.program_id(0)

    @pl.when(quarter == 0)
    def _():
        row = lax.broadcasted_iota(jnp.int32, (rows, channels), 0)
        low_edges, high_edges = ([], [], []), ([], [], [])
        for video in range(videos):
            span = slice(video * rows, (video + 1) * rows)
            one = slice(video, video + 1)
            main = part_ref[span, :]
            main = main + jnp.where(row == 0, low_in_ref[2, one, :], 0.0)
            main = main + jnp.where(row == rows - 1, high_in_ref[0, one, :], 0.0)
            low = part_ref[edges + video : edges + video + 1, :] + low_in_ref[1, one, :]
            high_at = edges + videos + video
            high = part_ref[high_at : high_at + 1, :] + high_in_ref[1, one, :]
            after = jnp.where(row == rows - 1, high, pltpu.roll(main, rows - 1, 0))
            before = jnp.where(row == 0, low, pltpu.roll(main, 1, 0))
            for index, part in enumerate((after, main, before)):
                windows_ref[index, span, :] = part.astype(jnp.bfloat16)
            for index, part in enumerate((main[:1], low, low_in_ref[0, one, :])):
                low_edges[index].append(part)
            for index, part in enumerate((high_in_ref[2, one, :], high, main[rows - 1 :])):
                high_edges[index].append(part)
        spare = [jnp.zeros((windows_ref.shape[1] - edges - 2 * videos, channels), jnp.float32)]
        for index in range(3):
            edge = jnp.concatenate(low_edges[index] + high_edges[index] + spare, axis=0)
            windows_ref[index, edges:, :] = edge.astype(jnp.bfloat16)

    total = jnp.zeros(share_ref.shape[1:], jnp.float32)
    for index in range(3):
        total = total + lax.dot_general(
            windows_ref[index],
            taps_ref[index],
            (((1,), (1,)), ((), ())),
            preferred_element_type=jnp.float32,
        )
    spare = jnp.zeros((windows_ref.shape[1] - edges - 2 * videos, width), jnp.float32)
    slope = jnp.concatenate(
        [
            silu_slope(pre_ref[...].astype(jnp.float32)),
            jnp.where(valid_ref[0] > 0, silu_slope(pre_low_ref[3]), 0.0),
            jnp.where(valid_ref[1] > 0, silu_slope(pre_high_ref[3]), 0.0),
            spare,
        ],
        axis=0,
    )
    pre_share_ref[0] = (total * slope).astype(jnp.bfloat16)
    lanes = pl.ds(pl.multiple_of(quarter * width, width), width)
    share_ref[0] = windows_ref[1, :, lanes]


def gradients(partial, from_low, from_high, filter_second, pre_rows, valid, quarters):
    lag_count, channels, _ = filter_second.shape
    rows, width = pre_rows.shape[0] + 16, channels // quarters
    edge_shape = from_low.shape
    share = jax.ShapeDtypeStruct((quarters, rows, width), jnp.bfloat16)
    share_spec = pl.BlockSpec((1, rows, width), lambda q: (q, 0, 0))
    edge_spec = pl.BlockSpec(edge_shape, lambda q: (0, 0, 0))
    edge_part = pl.BlockSpec(edge_shape[:2] + (width,), lambda q: (0, 0, q))
    return pl.pallas_call(
        grads_kernel,
        grid=(quarters,),
        out_shape=(share, share),
        in_specs=[
            pl.BlockSpec(memory_space=pltpu.SMEM),
            pl.BlockSpec(partial.shape, lambda q: (0, 0)),
            edge_spec,
            edge_spec,
            pl.BlockSpec((lag_count, width, channels), lambda q: (0, q, 0)),
            pl.BlockSpec((pre_rows.shape[0], width), lambda q: (0, q)),
            edge_part,
            edge_part,
        ],
        out_specs=(share_spec, share_spec),
        scratch_shapes=[pltpu.VMEM((lag_count, rows, channels), jnp.bfloat16)],
        compiler_params=pltpu.CompilerParams(vmem_limit_bytes=24 * 2**20),
        cost_estimate=pl.CostEstimate(
            flops=2 * rows * channels * channels * lag_count,
            bytes_accessed=12 * 2**20,
            transcendentals=rows * channels,
        ),
    )(valid, partial, from_low, from_high, filter_second, pre_rows, from_low, from_high)


def terms_kernel(videos, source_count, order_ref, grad_ref, input_ref, keep_ref, give_ref, lag_ref):
    width = grad_ref.shape[2]
    main = grad_ref.shape[1] - 16
    rows = main // videos
    groups, each, outs = keep_ref.shape
    core = order_ref[source_count]
    row = lax.broadcasted_iota(jnp.int32, (rows, width), 0)
    for source in range(source_count):
        at = order_ref[source]
        edges = grad_ref[at, main:, :].astype(jnp.float32)
        for video in range(videos):
            span = slice(video * rows, (video + 1) * rows)
            grad = grad_ref[at, span, :].astype(jnp.float32)
            low, high = edges[video : video + 1], edges[videos + video : videos + video + 1]
            after = jnp.where(row == rows - 1, high, pltpu.roll(grad, rows - 1, 0))
            before = jnp.where(row == 0, low, pltpu.roll(grad, 1, 0))
            for index, part in enumerate((after, grad, before)):
                lag_ref[
                    source * main + video * rows : source * main + (video + 1) * rows,
                    index * width : (index + 1) * width,
                ] = part.astype(jnp.bfloat16)
    channels = groups * 2 * each
    step = min(256, channels)
    for start in range(0, channels, step):
        total = lax.dot_general(
            input_ref[:, start : start + step],
            lag_ref[...],
            (((0,), (0,)), ((), ())),
            preferred_element_type=jnp.float32,
        )
        total = total.reshape(step // (2 * each), 2, each, outs)
        first, second = total[:, 0], total[:, 1]
        span = slice(start // (2 * each), (start + step) // (2 * each))
        keep_ref[span] = jnp.where(core == 0, first, second)
        give_ref[span] = jnp.where(core == 0, second, first).astype(jnp.bfloat16)


def filter_terms(inputs, gradient, order, videos, lag_count, each):
    source_count, block, width = gradient.shape
    channels = inputs.shape[-1]
    shape = (channels // (2 * each), each, lag_count * width)
    rows = source_count * (block - 16)
    vmem = pl.BlockSpec(memory_space=pltpu.VMEM)
    return pl.pallas_call(
        lambda *refs: terms_kernel(videos, source_count, *refs),
        out_shape=(
            jax.ShapeDtypeStruct(shape, jnp.float32),
            jax.ShapeDtypeStruct(shape, jnp.bfloat16),
        ),
        in_specs=[pl.BlockSpec(memory_space=pltpu.SMEM)] + [vmem] * 2,
        out_specs=(vmem, vmem),
        scratch_shapes=[pltpu.VMEM((rows, lag_count * width), jnp.bfloat16)],
        compiler_params=pltpu.CompilerParams(vmem_limit_bytes=20 * 2**20),
        cost_estimate=pl.CostEstimate(
            flops=2 * rows * channels * lag_count * width,
            bytes_accessed=10 * 2**20,
            transcendentals=0,
        ),
    )(order, gradient, inputs)


def share_by_core(keep, give):
    got = ring_shift(give, "core", 1)
    return (keep + got.astype(jnp.float32)).astype(jnp.bfloat16)


def sum_over_x(share):
    x_total, z_total = lax.axis_size("x"), lax.axis_size("z")
    groups, each, outs = share.shape
    share = exchange(share.reshape(x_total, z_total * each, outs), "x")
    return jnp.sum(share.astype(jnp.float32), axis=0).reshape(z_total, each, outs)


def on_device(bin_grad, tap_weight, tap_index, features, preact, filter_second):
    video_count, snip_count, channels = features.shape
    peers = lax.axis_size(TM)
    quarters = lax.axis_size("video")
    place, core = lax.axis_index("video"), lax.axis_index("core")
    lag_count = filter_second.shape[0]
    main_rows = video_count * snip_count
    each = channels // peers
    sent = send_slots(bin_grad, tap_weight, tap_index, snip_count, peers)
    got = exchange(sent, TM)

    pre_values = preact.astype(jnp.float32).reshape(main_rows, channels)
    activation = jax.nn.silu(pre_values).astype(jnp.bfloat16)
    act_all = lax.all_gather(activation, "video", axis=0, tiled=True)
    feature_all = lax.all_gather(
        features.reshape(main_rows, channels), "video", axis=0, tiled=True
    )

    partial = collect(got, channels, main_rows + 2 * video_count)
    ends = partial[:main_rows].reshape(video_count, snip_count, channels)
    low = partial[main_rows : main_rows + video_count]
    high = partial[main_rows + video_count :]
    pre_ends = pre_values.reshape(ends.shape)
    from_low = neighbours(jnp.stack([ends[:, -2], ends[:, -1], high, pre_ends[:, -1]]), True)
    from_high = neighbours(jnp.stack([low, ends[:, 0], ends[:, 1], pre_ends[:, 0]]), False)
    at = lax.axis_index(TM)
    valid = jnp.stack([at > 0, at < peers - 1]).astype(jnp.int32)
    pre_rows = preact.reshape(main_rows, channels)
    snippet_share, pre_share = gradients(
        partial, from_low, from_high, filter_second, pre_rows, valid, quarters
    )
    snippet_share = exchange(snippet_share, "video")
    pre_share = pre_share + snippet_share[0, 0, 0] * 0
    after_pre = (pre_share[0, 0, 0] * 0).astype(jnp.int32)
    pre_share = exchange(pre_share, "video")

    order = jnp.stack([jnp.int32(source) for source in range(quarters)] + [core])
    second = share_by_core(
        *filter_terms(act_all, snippet_share, order + after_pre, video_count, lag_count, each)
    )
    first = share_by_core(
        *filter_terms(feature_all, pre_share, order, video_count, lag_count, each)
    )
    second, first = sum_over_x(second), sum_over_x(first)
    both = jnp.stack([first, second], axis=1).astype(jnp.bfloat16)
    mine = jnp.sum(exchange(both, "z").astype(jnp.float32), axis=0)

    width = channels // quarters
    held = [mine] + [ring_shift(mine, "video", shift) for shift in range(1, quarters)]
    blocks = []
    for quarter in range(quarters):
        block = held[0]
        for shift in range(1, quarters):
            block = jnp.where((place - shift) % quarters == quarter, held[shift], block)
        blocks.append(block.reshape(2, -1, lag_count, width))
    whole = jnp.concatenate(blocks, axis=-1)
    return (whole[0], whole[1])


def solution(mesh):
    shape = (mesh.shape["video"],) + TM_SIZES
    fine = Mesh(np.asarray(mesh.devices).reshape(shape), ("video",) + TM)
    return jax.shard_map(
        on_device,
        mesh=fine,
        in_specs=(
            P("video", TM, None, None),
            P("video", TM, None, None),
            P("video", TM, None, None),
            P("video", TM, None),
            P("video", TM, None),
            P(),
        ),
        out_specs=(P(TM, None, None), P(TM, None, None)),
        check_vma=False,
    )
```

```python
import jax
import jax.numpy as jnp
import numpy as np
from jax import lax
from jax.experimental import pallas as pl
from jax.experimental.pallas import tpu as pltpu
from jax.sharding import Mesh
from jax.sharding import PartitionSpec as P

TM = ("x", "z", "core")
TM_SIZES = (4, 8, 2)
META = 128


def silu_slope(values):
    sigma = jax.nn.sigmoid(values)
    return sigma * (1.0 + values * (1.0 - sigma))


def neighbours(value, forward):
    count = lax.axis_size(TM)
    pairs = [(i, i + 1) for i in range(count - 1)]
    if not forward:
        pairs = [(j, i) for i, j in pairs]
    return lax.ppermute(value, TM, pairs)


def ring_shift(value, axis, shift):
    count = lax.axis_size(axis)
    return lax.ppermute(value, axis, [(i, (i + shift) % count) for i in range(count)])


def exchange(value, axis):
    return lax.all_to_all(value, axis, split_axis=0, concat_axis=0, tiled=True)


def route(first_tap, snip_count, unit_axis):
    count = first_tap[0].shape[0]
    col, row = first_tap
    mine, other = (col, row) if unit_axis == 0 else (row, col)
    reduce_axis = 1 - unit_axis
    block, block_other = mine // snip_count, other // snip_count
    crossing = mine % snip_count == snip_count - 1
    crossing_other = other % snip_count == snip_count - 1
    earlier = lax.broadcasted_iota(jnp.int32, (count, count), reduce_axis) < lax.broadcasted_iota(
        jnp.int32, (count, count), unit_axis
    )
    rank = jnp.sum(
        ((block == block_other) & crossing_other & earlier).astype(jnp.int32),
        axis=reduce_axis,
        keepdims=True,
    )
    target = block + (crossing & (rank % 2 == 1)).astype(jnp.int32)
    return target, mine - target * snip_count


def halved(value):
    high = lax.reduce_precision(value, 8, 7)
    rest = value - high
    middle = lax.reduce_precision(rest, 8, 7)
    return high, middle, rest - middle


def send_slots(bin_grad, tap_weight, tap_index, snip_count, peers):
    video_count, prop_count, bin_count, tap_count = tap_index.shape
    channels = bin_grad.shape[-1]
    units = video_count * prop_count * bin_count
    capacity = bin_count * ((video_count * prop_count + peers - 1) // peers)
    first = tap_index[..., 0].reshape(units)
    taps = (first[:, None], first[None, :])
    target_col, local = route(taps, snip_count, 0)
    target_row, _ = route(taps, snip_count, 1)
    earlier = lax.broadcasted_iota(jnp.int32, (units, units), 0) < lax.broadcasted_iota(
        jnp.int32, (units, units), 1
    )
    position = jnp.sum(
        ((target_col == target_row) & earlier).astype(jnp.int32), axis=0, keepdims=True
    )
    slot = target_row * capacity + position
    matches = (
        lax.broadcasted_iota(jnp.int32, (peers * capacity, units), 0) == slot
    ).astype(jnp.bfloat16)
    video = lax.broadcasted_iota(jnp.int32, (units, 1), 0) // (prop_count * bin_count)
    main = video_count * snip_count

    def line(step):
        at = local + step
        inside = video * snip_count + at
        edge = main + video + jnp.where(at < 0, 0, video_count)
        return jnp.where((at < 0) | (at >= snip_count), edge, inside)

    weights = tap_weight.reshape(units, tap_count)
    columns = []
    for step in range(2):
        where_to = line(step)
        columns += [(where_to // 256).astype(jnp.float32), (where_to % 256).astype(jnp.float32)]
        columns += list(halved(weights[:, step : step + 1]))
    lane = lax.broadcasted_iota(jnp.int32, (units, META), 1)
    meta = jnp.zeros((units, META), jnp.float32)
    for index, column in enumerate(columns):
        meta = jnp.where(lane == index, column, meta)
    payload = jnp.concatenate([bin_grad.reshape(units, channels), meta.astype(jnp.bfloat16)], axis=1)
    rows = jnp.dot(matches, payload, preferred_element_type=jnp.float32).astype(jnp.bfloat16)
    return rows.reshape(peers, capacity, channels + META)


def collect(got, channels, row_count):
    rows = got.reshape(-1, channels + META)
    grads = rows[:, :channels].astype(jnp.float32)
    meta = rows[:, channels:].astype(jnp.float32)
    meta_t = meta[:, :16].T
    total = jnp.zeros((row_count, channels), jnp.float32)
    for step in range(2):
        base = 5 * step
        where_to = (meta_t[base : base + 1] * 256.0 + meta_t[base + 1 : base + 2]).astype(jnp.int32)
        weight = meta[:, base + 2 : base + 3] + meta[:, base + 3 : base + 4] + meta[:, base + 4 : base + 5]
        tap_rows = (weight * grads).astype(jnp.bfloat16)
        table = (
            lax.broadcasted_iota(jnp.int32, (row_count, rows.shape[0]), 0) == where_to
        ).astype(jnp.bfloat16)
        total = total + jnp.dot(table, tap_rows, preferred_element_type=jnp.float32)
    return total


def grads_kernel(
    valid_ref,
    part_ref,
    low_in_ref,
    high_in_ref,
    taps_ref,
    pre_ref,
    pre_low_ref,
    pre_high_ref,
    share_ref,
    windows_ref,
):
    videos = low_in_ref.shape[1]
    width = share_ref.shape[3]
    edges = part_ref.shape[0] - 2 * videos
    rows = edges // videos
    channels = part_ref.shape[1]
    quarter = pl.program_id(0)

    @pl.when(quarter == 0)
    def _():
        row = lax.broadcasted_iota(jnp.int32, (rows, channels), 0)
        low_edges, high_edges = ([], [], []), ([], [], [])
        for video in range(videos):
            span = slice(video * rows, (video + 1) * rows)
            one = slice(video, video + 1)
            main = part_ref[span, :]
            main = main + jnp.where(row == 0, low_in_ref[2, one, :], 0.0)
            main = main + jnp.where(row == rows - 1, high_in_ref[0, one, :], 0.0)
            low = part_ref[edges + video : edges + video + 1, :] + low_in_ref[1, one, :]
            high_at = edges + videos + video
            high = part_ref[high_at : high_at + 1, :] + high_in_ref[1, one, :]
            after = jnp.where(row == rows - 1, high, pltpu.roll(main, rows - 1, 0))
            before = jnp.where(row == 0, low, pltpu.roll(main, 1, 0))
            for index, part in enumerate((after, main, before)):
                windows_ref[index, span, :] = part.astype(jnp.bfloat16)
            for index, part in enumerate((main[:1], low, low_in_ref[0, one, :])):
                low_edges[index].append(part)
            for index, part in enumerate((high_in_ref[2, one, :], high, main[rows - 1 :])):
                high_edges[index].append(part)
        spare = [jnp.zeros((windows_ref.shape[1] - edges - 2 * videos, channels), jnp.float32)]
        for index in range(3):
            edge = jnp.concatenate(low_edges[index] + high_edges[index] + spare, axis=0)
            windows_ref[index, edges:, :] = edge.astype(jnp.bfloat16)

    total = jnp.zeros(share_ref.shape[2:], jnp.float32)
    for index in range(3):
        total = total + lax.dot_general(
            windows_ref[index],
            taps_ref[index],
            (((1,), (1,)), ((), ())),
            preferred_element_type=jnp.float32,
        )
    spare = jnp.zeros((windows_ref.shape[1] - edges - 2 * videos, width), jnp.float32)
    slope = jnp.concatenate(
        [
            silu_slope(pre_ref[...].astype(jnp.float32)),
            jnp.where(valid_ref[0] > 0, silu_slope(pre_low_ref[3]), 0.0),
            jnp.where(valid_ref[1] > 0, silu_slope(pre_high_ref[3]), 0.0),
            spare,
        ],
        axis=0,
    )
    share_ref[0, 1] = (total * slope).astype(jnp.bfloat16)
    lanes = pl.ds(pl.multiple_of(quarter * width, width), width)
    share_ref[0, 0] = windows_ref[1, :, lanes]


def gradients(partial, from_low, from_high, filter_second, pre_rows, valid, quarters):
    lag_count, channels, _ = filter_second.shape
    rows, width = pre_rows.shape[0] + 16, channels // quarters
    edge_shape = from_low.shape
    share = jax.ShapeDtypeStruct((quarters, 2, rows, width), jnp.bfloat16)
    share_spec = pl.BlockSpec((1, 2, rows, width), lambda q: (q, 0, 0, 0))
    edge_spec = pl.BlockSpec(edge_shape, lambda q: (0, 0, 0))
    edge_part = pl.BlockSpec(edge_shape[:2] + (width,), lambda q: (0, 0, q))
    return pl.pallas_call(
        grads_kernel,
        grid=(quarters,),
        out_shape=share,
        in_specs=[
            pl.BlockSpec(memory_space=pltpu.SMEM),
            pl.BlockSpec(partial.shape, lambda q: (0, 0)),
            edge_spec,
            edge_spec,
            pl.BlockSpec((lag_count, width, channels), lambda q: (0, q, 0)),
            pl.BlockSpec((pre_rows.shape[0], width), lambda q: (0, q)),
            edge_part,
            edge_part,
        ],
        out_specs=share_spec,
        scratch_shapes=[pltpu.VMEM((lag_count, rows, channels), jnp.bfloat16)],
        compiler_params=pltpu.CompilerParams(vmem_limit_bytes=24 * 2**20),
        cost_estimate=pl.CostEstimate(
            flops=2 * rows * channels * channels * lag_count,
            bytes_accessed=12 * 2**20,
            transcendentals=rows * channels,
        ),
    )(valid, partial, from_low, from_high, filter_second, pre_rows, from_low, from_high)


def terms_kernel(videos, layer, order_ref, grad_ref, *refs):
    input_refs, (keep_ref, give_ref, lag_ref) = refs[:-3], refs[-3:]
    sources, width = grad_ref.shape[0], grad_ref.shape[3]
    main = grad_ref.shape[2] - 16
    rows = main // videos
    groups, each, outs = keep_ref.shape
    core = order_ref[0]
    row = lax.broadcasted_iota(jnp.int32, (rows, width), 0)
    for source in range(sources):
        edges = grad_ref[source, layer, main:, :].astype(jnp.float32)
        for video in range(videos):
            span = slice(video * rows, (video + 1) * rows)
            grad = grad_ref[source, layer, span, :].astype(jnp.float32)
            low, high = edges[video : video + 1], edges[videos + video : videos + video + 1]
            after = jnp.where(row == rows - 1, high, pltpu.roll(grad, rows - 1, 0))
            before = jnp.where(row == 0, low, pltpu.roll(grad, 1, 0))
            for index, part in enumerate((after, grad, before)):
                lag_ref[
                    source * main + video * rows : source * main + (video + 1) * rows,
                    index * width : (index + 1) * width,
                ] = part.astype(jnp.bfloat16)
    pieces = []
    gathered = input_refs[0].shape[0] // sources
    if gathered == main:
        pieces.append((input_refs[0], 0, sources * main, 0))
    else:
        for source in range(sources):
            pieces.append((input_refs[0], source * gathered, gathered, source * main))
        for index, ref in enumerate(input_refs[1:]):
            at = pl.multiple_of(order_ref[1 + index] * main + gathered, gathered)
            pieces.append((ref, 0, main - gathered, at))
    channels = groups * 2 * each
    step = min(256, channels)
    for start in range(0, channels, step):
        total = jnp.zeros((step, outs), jnp.float32)
        for ref, first, count, at in pieces:
            total = total + lax.dot_general(
                ref[first : first + count, start : start + step],
                lag_ref[pl.ds(at, count), :],
                (((0,), (0,)), ((), ())),
                preferred_element_type=jnp.float32,
            )
        total = total.reshape(step // (2 * each), 2, each, outs)
        first, second = total[:, 0], total[:, 1]
        span = slice(start // (2 * each), (start + step) // (2 * each))
        keep_ref[span] = jnp.where(core == 0, first, second)
        give_ref[span] = jnp.where(core == 0, second, first).astype(jnp.bfloat16)


def filter_terms(inputs, gradients, layer, order, videos, lag_count, each):
    sources, _, block, width = gradients.shape
    channels = inputs[0].shape[-1]
    shape = (channels // (2 * each), each, lag_count * width)
    rows = sources * (block - 16)
    vmem = pl.BlockSpec(memory_space=pltpu.VMEM)
    return pl.pallas_call(
        lambda *refs: terms_kernel(videos, layer, *refs),
        out_shape=(
            jax.ShapeDtypeStruct(shape, jnp.float32),
            jax.ShapeDtypeStruct(shape, jnp.bfloat16),
        ),
        in_specs=[pl.BlockSpec(memory_space=pltpu.SMEM)] + [vmem] * (1 + len(inputs)),
        out_specs=(vmem, vmem),
        scratch_shapes=[pltpu.VMEM((rows, lag_count * width), jnp.bfloat16)],
        compiler_params=pltpu.CompilerParams(vmem_limit_bytes=24 * 2**20),
        cost_estimate=pl.CostEstimate(
            flops=2 * rows * channels * lag_count * width,
            bytes_accessed=10 * 2**20,
            transcendentals=0,
        ),
    )(order, gradients, *inputs)


def share_by_core(keep, give):
    got = ring_shift(give, "core", 1)
    return (keep + got.astype(jnp.float32)).astype(jnp.bfloat16)


def on_device(bin_grad, tap_weight, tap_index, features, preact, filter_second):
    video_count, snip_count, channels = features.shape
    peers = lax.axis_size(TM)
    quarters = lax.axis_size("video")
    place, core = lax.axis_index("video"), lax.axis_index("core")
    lag_count = filter_second.shape[0]
    main_rows = video_count * snip_count
    each = channels // peers
    sent = send_slots(bin_grad, tap_weight, tap_index, snip_count, peers)
    got = exchange(sent, TM)

    pre_values = preact.astype(jnp.float32).reshape(main_rows, channels)
    activation = jax.nn.silu(pre_values).astype(jnp.bfloat16)
    act_all = lax.all_gather(activation, "video", axis=0, tiled=True)
    halves = features.reshape(2, main_rows // 2, channels)
    feature_all = [lax.all_gather(halves[0], "video", axis=0, tiled=True), halves[1]]
    for shift in range(1, quarters):
        feature_all.append(ring_shift(halves[1], "video", shift))

    partial = collect(got, channels, main_rows + 2 * video_count)
    ends = partial[:main_rows].reshape(video_count, snip_count, channels)
    low = partial[main_rows : main_rows + video_count]
    high = partial[main_rows + video_count :]
    arrived = sum(piece[0, 0] * 0 for piece in feature_all[2:]).astype(jnp.float32)
    pre_ends = pre_values.reshape(ends.shape)[:, :: snip_count - 1] + arrived
    from_low = neighbours(jnp.stack([ends[:, -2], ends[:, -1], high, pre_ends[:, 1]]), True)
    from_high = neighbours(jnp.stack([low, ends[:, 0], ends[:, 1], pre_ends[:, 0]]), False)
    at = lax.axis_index(TM)
    valid = jnp.stack([at > 0, at < peers - 1]).astype(jnp.int32)
    pre_rows = preact.reshape(main_rows, channels)
    shares = gradients(partial, from_low, from_high, filter_second, pre_rows, valid, quarters)
    block, width = shares.shape[2:]
    shares = exchange(shares.reshape(quarters, 2 * block, width), "video")
    shares = shares.reshape(quarters, 2, block, width)

    order = jnp.stack([core] + [(place + quarters - source) % quarters for source in range(quarters)])
    second = share_by_core(
        *filter_terms([act_all], shares, 0, order, video_count, lag_count, each)
    )
    first = share_by_core(
        *filter_terms(feature_all, shares, 1, order, video_count, lag_count, each)
    )
    x_total, z_total = lax.axis_size("x"), lax.axis_size("z")
    both = jnp.stack([part.reshape(x_total, -1, lag_count * width) for part in (first, second)], 1)
    both = exchange(both.reshape(x_total, -1, lag_count * width), "x")
    both = jnp.sum(both.astype(jnp.float32), axis=0).astype(jnp.bfloat16)
    both = both.reshape(2, z_total, each, lag_count * width).transpose(1, 0, 2, 3)
    mine = jnp.sum(exchange(both, "z").astype(jnp.float32), axis=0)

    held = [mine] + [ring_shift(mine, "video", shift) for shift in range(1, quarters)]
    blocks = []
    for quarter in range(quarters):
        block = held[0]
        for shift in range(1, quarters):
            block = jnp.where((place - shift) % quarters == quarter, held[shift], block)
        blocks.append(block.reshape(2, -1, lag_count, width))
    whole = jnp.concatenate(blocks, axis=-1)
    return (whole[0], whole[1])


def solution(mesh):
    shape = (mesh.shape["video"],) + TM_SIZES
    fine = Mesh(np.asarray(mesh.devices).reshape(shape), ("video",) + TM)
    return jax.shard_map(
        on_device,
        mesh=fine,
        in_specs=(
            P("video", TM, None, None),
            P("video", TM, None, None),
            P("video", TM, None, None),
            P("video", TM, None),
            P("video", TM, None),
            P(),
        ),
        out_specs=(P(TM, None, None), P(TM, None, None)),
        check_vma=False,
    )
```

```python
import jax
import jax.numpy as jnp
import numpy as np
from jax import lax
from jax.experimental import pallas as pl
from jax.experimental.pallas import tpu as pltpu
from jax.sharding import Mesh
from jax.sharding import PartitionSpec as P

TM = ("x", "z", "core")
TM_SIZES = (4, 8, 2)
META = 128


def silu_slope(values):
    sigma = jax.nn.sigmoid(values)
    return sigma * (1.0 + values * (1.0 - sigma))


def neighbours(value, forward):
    count = lax.axis_size(TM)
    pairs = [(i, i + 1) for i in range(count - 1)]
    if not forward:
        pairs = [(j, i) for i, j in pairs]
    return lax.ppermute(value, TM, pairs)


def ring_shift(value, axis, shift):
    count = lax.axis_size(axis)
    return lax.ppermute(value, axis, [(i, (i + shift) % count) for i in range(count)])


def around_video(rows):
    count = lax.axis_size("video")
    half = rows.shape[0] // 2
    if count != 4:
        held = [rows] + [ring_shift(rows, "video", shift) for shift in range(1, count)]
        return [piece for part in held for piece in (part[:half], part[half:])]
    below, above = ring_shift(rows, "video", 1), ring_shift(rows, "video", 3)
    far = [ring_shift(below[:half], "video", 1), ring_shift(above[half:], "video", 3)]
    return [rows, below] + far + [above]


def exchange(value, axis):
    return lax.all_to_all(value, axis, split_axis=0, concat_axis=0, tiled=True)


def route(first_tap, snip_count, unit_axis):
    count = first_tap[0].shape[0]
    col, row = first_tap
    mine, other = (col, row) if unit_axis == 0 else (row, col)
    reduce_axis = 1 - unit_axis
    block, block_other = mine // snip_count, other // snip_count
    crossing = mine % snip_count == snip_count - 1
    crossing_other = other % snip_count == snip_count - 1
    earlier = lax.broadcasted_iota(jnp.int32, (count, count), reduce_axis) < lax.broadcasted_iota(
        jnp.int32, (count, count), unit_axis
    )
    rank = jnp.sum(
        ((block == block_other) & crossing_other & earlier).astype(jnp.int32),
        axis=reduce_axis,
        keepdims=True,
    )
    target = block + (crossing & (rank % 2 == 1)).astype(jnp.int32)
    return target, mine - target * snip_count


def halved(value):
    high = lax.reduce_precision(value, 8, 7)
    rest = value - high
    middle = lax.reduce_precision(rest, 8, 7)
    return high, middle, rest - middle


def send_slots(bin_grad, tap_weight, tap_index, snip_count, peers):
    video_count, prop_count, bin_count, tap_count = tap_index.shape
    channels = bin_grad.shape[-1]
    units = video_count * prop_count * bin_count
    capacity = bin_count * ((video_count * prop_count + peers - 1) // peers)
    first = tap_index[..., 0].reshape(units)
    taps = (first[:, None], first[None, :])
    target_col, local = route(taps, snip_count, 0)
    target_row, _ = route(taps, snip_count, 1)
    earlier = lax.broadcasted_iota(jnp.int32, (units, units), 0) < lax.broadcasted_iota(
        jnp.int32, (units, units), 1
    )
    position = jnp.sum(
        ((target_col == target_row) & earlier).astype(jnp.int32), axis=0, keepdims=True
    )
    slot = target_row * capacity + position
    matches = (
        lax.broadcasted_iota(jnp.int32, (peers * capacity, units), 0) == slot
    ).astype(jnp.bfloat16)
    video = lax.broadcasted_iota(jnp.int32, (units, 1), 0) // (prop_count * bin_count)
    main = video_count * snip_count

    def line(step):
        at = local + step
        inside = video * snip_count + at
        edge = main + video + jnp.where(at < 0, 0, video_count)
        return jnp.where((at < 0) | (at >= snip_count), edge, inside)

    weights = tap_weight.reshape(units, tap_count)
    columns = []
    for step in range(2):
        where_to = line(step)
        columns += [(where_to // 256).astype(jnp.float32), (where_to % 256).astype(jnp.float32)]
        columns += list(halved(weights[:, step : step + 1]))
    lane = lax.broadcasted_iota(jnp.int32, (units, META), 1)
    meta = jnp.zeros((units, META), jnp.float32)
    for index, column in enumerate(columns):
        meta = jnp.where(lane == index, column, meta)
    payload = jnp.concatenate([bin_grad.reshape(units, channels), meta.astype(jnp.bfloat16)], axis=1)
    rows = jnp.dot(matches, payload, preferred_element_type=jnp.float32).astype(jnp.bfloat16)
    return rows.reshape(peers, capacity, channels + META)


def collect(got, channels, row_count):
    rows = got.reshape(-1, channels + META)
    grads = rows[:, :channels].astype(jnp.float32)
    meta = rows[:, channels:].astype(jnp.float32)
    meta_t = meta[:, :16].T
    total = jnp.zeros((row_count, channels), jnp.float32)
    for step in range(2):
        base = 5 * step
        where_to = (meta_t[base : base + 1] * 256.0 + meta_t[base + 1 : base + 2]).astype(jnp.int32)
        weight = meta[:, base + 2 : base + 3] + meta[:, base + 3 : base + 4] + meta[:, base + 4 : base + 5]
        tap_rows = (weight * grads).astype(jnp.bfloat16)
        table = (
            lax.broadcasted_iota(jnp.int32, (row_count, rows.shape[0]), 0) == where_to
        ).astype(jnp.bfloat16)
        total = total + jnp.dot(table, tap_rows, preferred_element_type=jnp.float32)
    return total


def grads_kernel(
    valid_ref,
    part_ref,
    low_in_ref,
    high_in_ref,
    taps_ref,
    pre_ref,
    pre_low_ref,
    pre_high_ref,
    share_ref,
    windows_ref,
):
    videos = low_in_ref.shape[1]
    width = share_ref.shape[3]
    edges = part_ref.shape[0] - 2 * videos
    rows = edges // videos
    channels = part_ref.shape[1]
    quarter = pl.program_id(0)

    @pl.when(quarter == 0)
    def _():
        row = lax.broadcasted_iota(jnp.int32, (rows, channels), 0)
        low_edges, high_edges = ([], [], []), ([], [], [])
        for video in range(videos):
            span = slice(video * rows, (video + 1) * rows)
            one = slice(video, video + 1)
            main = part_ref[span, :]
            main = main + jnp.where(row == 0, low_in_ref[2, one, :], 0.0)
            main = main + jnp.where(row == rows - 1, high_in_ref[0, one, :], 0.0)
            low = part_ref[edges + video : edges + video + 1, :] + low_in_ref[1, one, :]
            high_at = edges + videos + video
            high = part_ref[high_at : high_at + 1, :] + high_in_ref[1, one, :]
            after = jnp.where(row == rows - 1, high, pltpu.roll(main, rows - 1, 0))
            before = jnp.where(row == 0, low, pltpu.roll(main, 1, 0))
            for index, part in enumerate((after, main, before)):
                windows_ref[index, span, :] = part.astype(jnp.bfloat16)
            for index, part in enumerate((main[:1], low, low_in_ref[0, one, :])):
                low_edges[index].append(part)
            for index, part in enumerate((high_in_ref[2, one, :], high, main[rows - 1 :])):
                high_edges[index].append(part)
        spare = [jnp.zeros((windows_ref.shape[1] - edges - 2 * videos, channels), jnp.float32)]
        for index in range(3):
            edge = jnp.concatenate(low_edges[index] + high_edges[index] + spare, axis=0)
            windows_ref[index, edges:, :] = edge.astype(jnp.bfloat16)

    total = jnp.zeros(share_ref.shape[2:], jnp.float32)
    for index in range(3):
        total = total + lax.dot_general(
            windows_ref[index],
            taps_ref[index],
            (((1,), (1,)), ((), ())),
            preferred_element_type=jnp.float32,
        )
    spare = jnp.zeros((windows_ref.shape[1] - edges - 2 * videos, width), jnp.float32)
    slope = jnp.concatenate(
        [
            silu_slope(pre_ref[...].astype(jnp.float32)),
            jnp.where(valid_ref[0] > 0, silu_slope(pre_low_ref[3]), 0.0),
            jnp.where(valid_ref[1] > 0, silu_slope(pre_high_ref[3]), 0.0),
            spare,
        ],
        axis=0,
    )
    share_ref[0, 1] = (total * slope).astype(jnp.bfloat16)
    lanes = pl.ds(pl.multiple_of(quarter * width, width), width)
    share_ref[0, 0] = windows_ref[1, :, lanes]


def gradients(partial, from_low, from_high, filter_second, pre_rows, valid, quarters):
    lag_count, channels, _ = filter_second.shape
    rows, width = pre_rows.shape[0] + 16, channels // quarters
    edge_shape = from_low.shape
    share = jax.ShapeDtypeStruct((quarters, 2, rows, width), jnp.bfloat16)
    share_spec = pl.BlockSpec((1, 2, rows, width), lambda q: (q, 0, 0, 0))
    edge_spec = pl.BlockSpec(edge_shape, lambda q: (0, 0, 0))
    edge_part = pl.BlockSpec(edge_shape[:2] + (width,), lambda q: (0, 0, q))
    return pl.pallas_call(
        grads_kernel,
        grid=(quarters,),
        out_shape=share,
        in_specs=[
            pl.BlockSpec(memory_space=pltpu.SMEM),
            pl.BlockSpec(partial.shape, lambda q: (0, 0)),
            edge_spec,
            edge_spec,
            pl.BlockSpec((lag_count, width, channels), lambda q: (0, q, 0)),
            pl.BlockSpec((pre_rows.shape[0], width), lambda q: (0, q)),
            edge_part,
            edge_part,
        ],
        out_specs=share_spec,
        scratch_shapes=[pltpu.VMEM((lag_count, rows, channels), jnp.bfloat16)],
        compiler_params=pltpu.CompilerParams(vmem_limit_bytes=24 * 2**20),
        cost_estimate=pl.CostEstimate(
            flops=2 * rows * channels * channels * lag_count,
            bytes_accessed=12 * 2**20,
            transcendentals=rows * channels,
        ),
    )(valid, partial, from_low, from_high, filter_second, pre_rows, from_low, from_high)


def terms_kernel(videos, layer, order_ref, grad_ref, *refs):
    input_refs, (keep_ref, give_ref, lag_ref) = refs[:-3], refs[-3:]
    sources, width = grad_ref.shape[0], grad_ref.shape[3]
    main = grad_ref.shape[2] - 16
    rows = main // videos
    _, each, outs = keep_ref.shape
    core = order_ref[0]

    @pl.when(pl.program_id(0) == 0)
    def _():
        row = lax.broadcasted_iota(jnp.int32, (rows, width), 0)
        for source in range(sources):
            at = order_ref[1 + source]
            edges = grad_ref[at, layer, main:, :].astype(jnp.float32)
            for video in range(videos):
                span = slice(video * rows, (video + 1) * rows)
                grad = grad_ref[at, layer, span, :].astype(jnp.float32)
                low, high = edges[video : video + 1], edges[videos + video : videos + video + 1]
                after = jnp.where(row == rows - 1, high, pltpu.roll(grad, rows - 1, 0))
                before = jnp.where(row == 0, low, pltpu.roll(grad, 1, 0))
                for index, part in enumerate((after, grad, before)):
                    lag_ref[
                        source * main + video * rows : source * main + (video + 1) * rows,
                        index * width : (index + 1) * width,
                    ] = part.astype(jnp.bfloat16)

    total = jnp.zeros((input_refs[0].shape[1], outs), jnp.float32)
    offset = 0
    for ref in input_refs:
        total = total + lax.dot_general(
            ref[...],
            lag_ref[offset : offset + ref.shape[0], :],
            (((0,), (0,)), ((), ())),
            preferred_element_type=jnp.float32,
        )
        offset += ref.shape[0]
    total = total.reshape(-1, 2, each, outs)
    first, second = total[:, 0], total[:, 1]
    keep_ref[...] = jnp.where(core == 0, first, second)
    give_ref[...] = jnp.where(core == 0, second, first).astype(jnp.bfloat16)


def filter_terms(inputs, gradients, layer, order, videos, lag_count, each):
    sources, _, block, width = gradients.shape
    channels = inputs[0].shape[-1]
    shape = (channels // (2 * each), each, lag_count * width)
    rows = sources * (block - 16)
    step = min(256, channels)
    out_spec = pl.BlockSpec((step // (2 * each),) + shape[1:], lambda i: (i, 0, 0))
    return pl.pallas_call(
        lambda *refs: terms_kernel(videos, layer, *refs),
        grid=(channels // step,),
        out_shape=(
            jax.ShapeDtypeStruct(shape, jnp.float32),
            jax.ShapeDtypeStruct(shape, jnp.bfloat16),
        ),
        in_specs=[
            pl.BlockSpec(memory_space=pltpu.SMEM),
            pl.BlockSpec(gradients.shape, lambda i: (0, 0, 0, 0)),
        ]
        + [pl.BlockSpec((piece.shape[0], step), lambda i: (0, i)) for piece in inputs],
        out_specs=(out_spec, out_spec),
        scratch_shapes=[pltpu.VMEM((rows, lag_count * width), jnp.bfloat16)],
        compiler_params=pltpu.CompilerParams(vmem_limit_bytes=24 * 2**20),
        cost_estimate=pl.CostEstimate(
            flops=2 * rows * channels * lag_count * width,
            bytes_accessed=10 * 2**20,
            transcendentals=0,
        ),
    )(order, gradients, *inputs)


def share_by_core(keep, give):
    got = ring_shift(give, "core", 1)
    return (keep + got.astype(jnp.float32)).astype(jnp.bfloat16)


def on_device(bin_grad, tap_weight, tap_index, features, preact, filter_second):
    video_count, snip_count, channels = features.shape
    peers = lax.axis_size(TM)
    quarters = lax.axis_size("video")
    place, core = lax.axis_index("video"), lax.axis_index("core")
    lag_count = filter_second.shape[0]
    main_rows = video_count * snip_count
    each = channels // peers
    sent = send_slots(bin_grad, tap_weight, tap_index, snip_count, peers)
    got = exchange(sent, TM)

    pre_values = preact.astype(jnp.float32).reshape(main_rows, channels)
    activation = jax.nn.silu(pre_values).astype(jnp.bfloat16)
    act_all = lax.all_gather(activation, "video", axis=0, tiled=True)
    feature_all = around_video(features.reshape(main_rows, channels))

    partial = collect(got, channels, main_rows + 2 * video_count)
    ends = partial[:main_rows].reshape(video_count, snip_count, channels)
    low = partial[main_rows : main_rows + video_count]
    high = partial[main_rows + video_count :]
    arrived = sum(piece[0, 0] * 0 for piece in feature_all[1:]).astype(jnp.float32)
    pre_ends = pre_values.reshape(ends.shape)[:, :: snip_count - 1] + arrived
    from_low = neighbours(jnp.stack([ends[:, -2], ends[:, -1], high, pre_ends[:, 1]]), True)
    from_high = neighbours(jnp.stack([low, ends[:, 0], ends[:, 1], pre_ends[:, 0]]), False)
    at = lax.axis_index(TM)
    valid = jnp.stack([at > 0, at < peers - 1]).astype(jnp.int32)
    pre_rows = preact.reshape(main_rows, channels)
    shares = gradients(partial, from_low, from_high, filter_second, pre_rows, valid, quarters)
    block, width = shares.shape[2:]
    shares = exchange(shares.reshape(quarters, 2 * block, width), "video")
    shares = shares.reshape(quarters, 2, block, width)

    in_order = jnp.stack([core] + [jnp.int32(source) for source in range(quarters)])
    around = jnp.stack([core] + [(place + quarters - source) % quarters for source in range(quarters)])
    second = share_by_core(
        *filter_terms([act_all], shares, 0, in_order, video_count, lag_count, each)
    )
    first = share_by_core(
        *filter_terms(feature_all, shares, 1, around, video_count, lag_count, each)
    )
    x_total, z_total = lax.axis_size("x"), lax.axis_size("z")
    both = jnp.stack([part.reshape(x_total, -1, lag_count * width) for part in (first, second)], 1)
    both = exchange(both.reshape(x_total, -1, lag_count * width), "x")
    both = jnp.sum(both.astype(jnp.float32), axis=0).astype(jnp.bfloat16)
    both = both.reshape(2, z_total, each, lag_count * width).transpose(1, 0, 2, 3)
    mine = jnp.sum(exchange(both, "z").astype(jnp.float32), axis=0)

    held = [mine] + [ring_shift(mine, "video", shift) for shift in range(1, quarters)]
    blocks = []
    for quarter in range(quarters):
        block = held[0]
        for shift in range(1, quarters):
            block = jnp.where((place - shift) % quarters == quarter, held[shift], block)
        blocks.append(block.reshape(2, -1, lag_count, width))
    whole = jnp.concatenate(blocks, axis=-1)
    return (whole[0], whole[1])


def solution(mesh):
    shape = (mesh.shape["video"],) + TM_SIZES
    fine = Mesh(np.asarray(mesh.devices).reshape(shape), ("video",) + TM)
    return jax.shard_map(
        on_device,
        mesh=fine,
        in_specs=(
            P("video", TM, None, None),
            P("video", TM, None, None),
            P("video", TM, None, None),
            P("video", TM, None),
            P("video", TM, None),
            P(),
        ),
        out_specs=(P(TM, None, None), P(TM, None, None)),
        check_vma=False,
    )
```

```python
import jax
import jax.numpy as jnp
import numpy as np
from jax import lax
from jax.experimental import pallas as pl
from jax.experimental.pallas import tpu as pltpu
from jax.sharding import Mesh
from jax.sharding import PartitionSpec as P

TM = ("x", "z", "core")
TM_SIZES = (4, 8, 2)
META = 128


def silu_slope(values):
    sigma = jax.nn.sigmoid(values)
    return sigma * (1.0 + values * (1.0 - sigma))


def neighbours(value, forward):
    count = lax.axis_size(TM)
    pairs = [(i, i + 1) for i in range(count - 1)]
    if not forward:
        pairs = [(j, i) for i, j in pairs]
    return lax.ppermute(value, TM, pairs)


def ring_shift(value, axis, shift):
    count = lax.axis_size(axis)
    return lax.ppermute(value, axis, [(i, (i + shift) % count) for i in range(count)])


def around_video(rows):
    count = lax.axis_size("video")
    half = rows.shape[0] // 2
    if count != 4:
        held = [rows] + [ring_shift(rows, "video", shift) for shift in range(1, count)]
        return [piece for part in held for piece in (part[:half], part[half:])]
    below, above = ring_shift(rows, "video", 1), ring_shift(rows, "video", 3)
    far = [ring_shift(below[:half], "video", 1), ring_shift(above[half:], "video", 3)]
    return [rows, below] + far + [above]


def exchange(value, axis):
    return lax.all_to_all(value, axis, split_axis=0, concat_axis=0, tiled=True)


def route(first_tap, snip_count, unit_axis):
    count = first_tap[0].shape[0]
    col, row = first_tap
    mine, other = (col, row) if unit_axis == 0 else (row, col)
    reduce_axis = 1 - unit_axis
    block, block_other = mine // snip_count, other // snip_count
    crossing = mine % snip_count == snip_count - 1
    crossing_other = other % snip_count == snip_count - 1
    earlier = lax.broadcasted_iota(jnp.int32, (count, count), reduce_axis) < lax.broadcasted_iota(
        jnp.int32, (count, count), unit_axis
    )
    rank = jnp.sum(
        ((block == block_other) & crossing_other & earlier).astype(jnp.int32),
        axis=reduce_axis,
        keepdims=True,
    )
    target = block + (crossing & (rank % 2 == 1)).astype(jnp.int32)
    return target, mine - target * snip_count


def halved(value):
    high = lax.reduce_precision(value, 8, 7)
    rest = value - high
    middle = lax.reduce_precision(rest, 8, 7)
    return high, middle, rest - middle


def send_slots(bin_grad, tap_weight, tap_index, snip_count, peers):
    video_count, prop_count, bin_count, tap_count = tap_index.shape
    channels = bin_grad.shape[-1]
    units = video_count * prop_count * bin_count
    capacity = bin_count * ((video_count * prop_count + peers - 1) // peers)
    first = tap_index[..., 0].reshape(units)
    taps = (first[:, None], first[None, :])
    target_col, local = route(taps, snip_count, 0)
    target_row, _ = route(taps, snip_count, 1)
    earlier = lax.broadcasted_iota(jnp.int32, (units, units), 0) < lax.broadcasted_iota(
        jnp.int32, (units, units), 1
    )
    position = jnp.sum(
        ((target_col == target_row) & earlier).astype(jnp.int32), axis=0, keepdims=True
    )
    slot = target_row * capacity + position
    matches = (
        lax.broadcasted_iota(jnp.int32, (peers * capacity, units), 0) == slot
    ).astype(jnp.bfloat16)
    video = lax.broadcasted_iota(jnp.int32, (units, 1), 0) // (prop_count * bin_count)
    main = video_count * snip_count

    def line(step):
        at = local + step
        inside = video * snip_count + at
        edge = main + video + jnp.where(at < 0, 0, video_count)
        return jnp.where((at < 0) | (at >= snip_count), edge, inside)

    weights = tap_weight.reshape(units, tap_count)
    columns = []
    for step in range(2):
        where_to = line(step)
        columns += [(where_to // 256).astype(jnp.float32), (where_to % 256).astype(jnp.float32)]
        columns += list(halved(weights[:, step : step + 1]))
    lane = lax.broadcasted_iota(jnp.int32, (units, META), 1)
    meta = jnp.zeros((units, META), jnp.float32)
    for index, column in enumerate(columns):
        meta = jnp.where(lane == index, column, meta)
    payload = jnp.concatenate([bin_grad.reshape(units, channels), meta.astype(jnp.bfloat16)], axis=1)
    rows = jnp.dot(matches, payload, preferred_element_type=jnp.float32).astype(jnp.bfloat16)
    return rows.reshape(peers, capacity, channels + META)


def collect_kernel(grad_ref, meta_ref, out_ref, table_ref):
    meta = meta_ref[...].astype(jnp.float32)

    @pl.when(pl.program_id(0) == 0)
    def _():
        across = meta.T
        row = lax.broadcasted_iota(jnp.int32, table_ref.shape[1:], 0)
        for step in range(2):
            base = 5 * step
            where_to = across[base : base + 1] * 256.0 + across[base + 1 : base + 2]
            hit = row == where_to.astype(jnp.int32)
            table_ref[step] = jnp.where(hit, 1.0, 0.0).astype(jnp.bfloat16)

    grads = grad_ref[...].astype(jnp.float32)
    total = jnp.zeros(out_ref.shape, jnp.float32)
    for step in range(2):
        base = 5 * step + 2
        weight = meta[:, base : base + 1] + meta[:, base + 1 : base + 2] + meta[:, base + 2 : base + 3]
        tap_rows = (weight * grads).astype(jnp.bfloat16)
        total = total + jnp.dot(table_ref[step], tap_rows, preferred_element_type=jnp.float32)
    out_ref[...] = total


def collect(got, channels, row_count):
    rows = got.reshape(-1, channels + META)
    slots = rows.shape[0]
    step = min(256, channels)
    return pl.pallas_call(
        collect_kernel,
        grid=(channels // step,),
        out_shape=jax.ShapeDtypeStruct((row_count, channels), jnp.float32),
        in_specs=[
            pl.BlockSpec((slots, step), lambda q: (0, q)),
            pl.BlockSpec((slots, META), lambda q: (0, channels // META)),
        ],
        out_specs=pl.BlockSpec((row_count, step), lambda q: (0, q)),
        scratch_shapes=[pltpu.VMEM((2, row_count, slots), jnp.bfloat16)],
        compiler_params=pltpu.CompilerParams(vmem_limit_bytes=20 * 2**20),
        cost_estimate=pl.CostEstimate(
            flops=4 * row_count * channels * slots,
            bytes_accessed=5 * 2**20,
            transcendentals=0,
        ),
    )(rows, rows)


def grads_kernel(
    valid_ref,
    part_ref,
    low_in_ref,
    high_in_ref,
    taps_ref,
    pre_ref,
    pre_low_ref,
    pre_high_ref,
    share_ref,
    windows_ref,
):
    videos = low_in_ref.shape[1]
    width = share_ref.shape[3]
    edges = windows_ref.shape[1] - 16
    rows = edges // videos
    channels = part_ref.shape[1]
    quarter = pl.program_id(0)

    @pl.when(quarter == 0)
    def _():
        row = lax.broadcasted_iota(jnp.int32, (rows, channels), 0)
        low_edges, high_edges = ([], [], []), ([], [], [])
        for video in range(videos):
            span = slice(video * rows, (video + 1) * rows)
            one = slice(video, video + 1)
            main = part_ref[span, :]
            main = main + jnp.where(row == 0, low_in_ref[2, one, :], 0.0)
            main = main + jnp.where(row == rows - 1, high_in_ref[0, one, :], 0.0)
            low = part_ref[edges + video : edges + video + 1, :] + low_in_ref[1, one, :]
            high_at = edges + videos + video
            high = part_ref[high_at : high_at + 1, :] + high_in_ref[1, one, :]
            after = jnp.where(row == rows - 1, high, pltpu.roll(main, rows - 1, 0))
            before = jnp.where(row == 0, low, pltpu.roll(main, 1, 0))
            for index, part in enumerate((after, main, before)):
                windows_ref[index, span, :] = part.astype(jnp.bfloat16)
            for index, part in enumerate((main[:1], low, low_in_ref[0, one, :])):
                low_edges[index].append(part)
            for index, part in enumerate((high_in_ref[2, one, :], high, main[rows - 1 :])):
                high_edges[index].append(part)
        spare = [jnp.zeros((windows_ref.shape[1] - edges - 2 * videos, channels), jnp.float32)]
        for index in range(3):
            edge = jnp.concatenate(low_edges[index] + high_edges[index] + spare, axis=0)
            windows_ref[index, edges:, :] = edge.astype(jnp.bfloat16)

    total = jnp.zeros(share_ref.shape[2:], jnp.float32)
    for index in range(3):
        total = total + lax.dot_general(
            windows_ref[index],
            taps_ref[index],
            (((1,), (1,)), ((), ())),
            preferred_element_type=jnp.float32,
        )
    spare = jnp.zeros((windows_ref.shape[1] - edges - 2 * videos, width), jnp.float32)
    slope = jnp.concatenate(
        [
            silu_slope(pre_ref[...].astype(jnp.float32)),
            jnp.where(valid_ref[0] > 0, silu_slope(pre_low_ref[3]), 0.0),
            jnp.where(valid_ref[1] > 0, silu_slope(pre_high_ref[3]), 0.0),
            spare,
        ],
        axis=0,
    )
    share_ref[0, 1] = (total * slope).astype(jnp.bfloat16)
    lanes = pl.ds(pl.multiple_of(quarter * width, width), width)
    share_ref[0, 0] = windows_ref[1, :, lanes]


def gradients(partial, from_low, from_high, filter_second, pre_rows, valid, quarters):
    lag_count, channels, _ = filter_second.shape
    rows, width = pre_rows.shape[0] + 16, channels // quarters
    edge_shape = from_low.shape
    share = jax.ShapeDtypeStruct((quarters, 2, rows, width), jnp.bfloat16)
    share_spec = pl.BlockSpec((1, 2, rows, width), lambda q: (q, 0, 0, 0))
    edge_spec = pl.BlockSpec(edge_shape, lambda q: (0, 0, 0))
    edge_part = pl.BlockSpec(edge_shape[:2] + (width,), lambda q: (0, 0, q))
    return pl.pallas_call(
        grads_kernel,
        grid=(quarters,),
        out_shape=share,
        in_specs=[
            pl.BlockSpec(memory_space=pltpu.SMEM),
            pl.BlockSpec(partial.shape, lambda q: (0, 0)),
            edge_spec,
            edge_spec,
            pl.BlockSpec((lag_count, width, channels), lambda q: (0, q, 0)),
            pl.BlockSpec((pre_rows.shape[0], width), lambda q: (0, q)),
            edge_part,
            edge_part,
        ],
        out_specs=share_spec,
        scratch_shapes=[pltpu.VMEM((lag_count, rows, channels), jnp.bfloat16)],
        compiler_params=pltpu.CompilerParams(vmem_limit_bytes=24 * 2**20),
        cost_estimate=pl.CostEstimate(
            flops=2 * rows * channels * channels * lag_count,
            bytes_accessed=12 * 2**20,
            transcendentals=rows * channels,
        ),
    )(valid, partial, from_low, from_high, filter_second, pre_rows, from_low, from_high)


def terms_kernel(videos, layer, order_ref, grad_ref, *refs):
    input_refs, (keep_ref, give_ref, lag_ref) = refs[:-3], refs[-3:]
    sources, width = grad_ref.shape[0], grad_ref.shape[3]
    main = grad_ref.shape[2] - 16
    rows = main // videos
    _, each, outs = keep_ref.shape
    core = order_ref[0]

    @pl.when(pl.program_id(0) == 0)
    def _():
        row = lax.broadcasted_iota(jnp.int32, (rows, width), 0)
        for source in range(sources):
            at = order_ref[1 + source]
            edges = grad_ref[at, layer, main:, :].astype(jnp.float32)
            for video in range(videos):
                span = slice(video * rows, (video + 1) * rows)
                grad = grad_ref[at, layer, span, :].astype(jnp.float32)
                low, high = edges[video : video + 1], edges[videos + video : videos + video + 1]
                after = jnp.where(row == rows - 1, high, pltpu.roll(grad, rows - 1, 0))
                before = jnp.where(row == 0, low, pltpu.roll(grad, 1, 0))
                for index, part in enumerate((after, grad, before)):
                    lag_ref[
                        source * main + video * rows : source * main + (video + 1) * rows,
                        index * width : (index + 1) * width,
                    ] = part.astype(jnp.bfloat16)

    total = jnp.zeros((input_refs[0].shape[1], outs), jnp.float32)
    offset = 0
    for ref in input_refs:
        total = total + lax.dot_general(
            ref[...],
            lag_ref[offset : offset + ref.shape[0], :],
            (((0,), (0,)), ((), ())),
            preferred_element_type=jnp.float32,
        )
        offset += ref.shape[0]
    total = total.reshape(-1, 2, each, outs)
    first, second = total[:, 0], total[:, 1]
    keep_ref[...] = jnp.where(core == 0, first, second)
    give_ref[...] = jnp.where(core == 0, second, first).astype(jnp.bfloat16)


def filter_terms(inputs, gradients, layer, order, videos, lag_count, each):
    sources, _, block, width = gradients.shape
    channels = inputs[0].shape[-1]
    shape = (channels // (2 * each), each, lag_count * width)
    rows = sources * (block - 16)
    step = min(256, channels)
    out_spec = pl.BlockSpec((step // (2 * each),) + shape[1:], lambda i: (i, 0, 0))
    return pl.pallas_call(
        lambda *refs: terms_kernel(videos, layer, *refs),
        grid=(channels // step,),
        out_shape=(
            jax.ShapeDtypeStruct(shape, jnp.float32),
            jax.ShapeDtypeStruct(shape, jnp.bfloat16),
        ),
        in_specs=[
            pl.BlockSpec(memory_space=pltpu.SMEM),
            pl.BlockSpec(gradients.shape, lambda i: (0, 0, 0, 0)),
        ]
        + [pl.BlockSpec((piece.shape[0], step), lambda i: (0, i)) for piece in inputs],
        out_specs=(out_spec, out_spec),
        scratch_shapes=[pltpu.VMEM((rows, lag_count * width), jnp.bfloat16)],
        compiler_params=pltpu.CompilerParams(vmem_limit_bytes=24 * 2**20),
        cost_estimate=pl.CostEstimate(
            flops=2 * rows * channels * lag_count * width,
            bytes_accessed=10 * 2**20,
            transcendentals=0,
        ),
    )(order, gradients, *inputs)


def share_by_core(keep, give):
    got = ring_shift(give, "core", 1)
    return (keep + got.astype(jnp.float32)).astype(jnp.bfloat16)


def on_device(bin_grad, tap_weight, tap_index, features, preact, filter_second):
    video_count, snip_count, channels = features.shape
    peers = lax.axis_size(TM)
    quarters = lax.axis_size("video")
    place, core = lax.axis_index("video"), lax.axis_index("core")
    lag_count = filter_second.shape[0]
    main_rows = video_count * snip_count
    each = channels // peers
    pre_values = preact.astype(jnp.float32).reshape(main_rows, channels)
    activation = jax.nn.silu(pre_values).astype(jnp.bfloat16)
    tap_weight = tap_weight + (activation[0, 0] * 0).astype(jnp.float32)
    sent = send_slots(bin_grad, tap_weight, tap_index, snip_count, peers)
    got = exchange(sent, TM)

    act_all = lax.all_gather(activation, "video", axis=0, tiled=True)
    feature_all = around_video(features.reshape(main_rows, channels))

    partial = collect(got, channels, main_rows + 16)
    ends = partial[:main_rows].reshape(video_count, snip_count, channels)
    low = partial[main_rows : main_rows + video_count]
    high = partial[main_rows + video_count : main_rows + 2 * video_count]
    arrived = sum(piece[0, 0] * 0 for piece in feature_all[2:4]).astype(jnp.float32)
    pre_ends = pre_values.reshape(ends.shape)[:, :: snip_count - 1] + arrived
    from_low = neighbours(jnp.stack([ends[:, -2], ends[:, -1], high, pre_ends[:, 1]]), True)
    from_high = neighbours(jnp.stack([low, ends[:, 0], ends[:, 1], pre_ends[:, 0]]), False)
    at = lax.axis_index(TM)
    valid = jnp.stack([at > 0, at < peers - 1]).astype(jnp.int32)
    pre_rows = preact.reshape(main_rows, channels)
    shares = gradients(partial, from_low, from_high, filter_second, pre_rows, valid, quarters)
    block, width = shares.shape[2:]
    shares = exchange(shares.reshape(quarters, 2 * block, width), "video")
    shares = shares.reshape(quarters, 2, block, width)

    in_order = jnp.stack([core] + [jnp.int32(source) for source in range(quarters)])
    around = jnp.stack([core] + [(place + quarters - source) % quarters for source in range(quarters)])
    second = share_by_core(
        *filter_terms([act_all], shares, 0, in_order, video_count, lag_count, each)
    )
    first = share_by_core(
        *filter_terms(feature_all, shares, 1, around, video_count, lag_count, each)
    )
    x_total, z_total = lax.axis_size("x"), lax.axis_size("z")
    both = jnp.stack([part.reshape(x_total, -1, lag_count * width) for part in (first, second)], 1)
    both = exchange(both.reshape(x_total, -1, lag_count * width), "x")
    both = jnp.sum(both.astype(jnp.float32), axis=0).astype(jnp.bfloat16)
    both = both.reshape(2, z_total, each, lag_count * width).transpose(1, 0, 2, 3)
    mine = jnp.sum(exchange(both, "z").astype(jnp.float32), axis=0)

    held = [mine] + [ring_shift(mine, "video", shift) for shift in range(1, quarters)]
    blocks = []
    for quarter in range(quarters):
        block = held[0]
        for shift in range(1, quarters):
            block = jnp.where((place - shift) % quarters == quarter, held[shift], block)
        blocks.append(block.reshape(2, -1, lag_count, width))
    whole = jnp.concatenate(blocks, axis=-1)
    return (whole[0], whole[1])


def solution(mesh):
    shape = (mesh.shape["video"],) + TM_SIZES
    fine = Mesh(np.asarray(mesh.devices).reshape(shape), ("video",) + TM)
    return jax.shard_map(
        on_device,
        mesh=fine,
        in_specs=(
            P("video", TM, None, None),
            P("video", TM, None, None),
            P("video", TM, None, None),
            P("video", TM, None),
            P("video", TM, None),
            P(),
        ),
        out_specs=(P(TM, None, None), P(TM, None, None)),
        check_vma=False,
    )
```

```python
import jax
import jax.numpy as jnp
import numpy as np
from jax import lax
from jax.experimental import pallas as pl
from jax.experimental.pallas import tpu as pltpu
from jax.sharding import Mesh
from jax.sharding import PartitionSpec as P

TM = ("x", "z", "core")
TM_SIZES = (4, 8, 2)
META = 128


def silu_slope(values):
    sigma = jax.nn.sigmoid(values)
    return sigma * (1.0 + values * (1.0 - sigma))


def neighbours(value, forward):
    count = lax.axis_size(TM)
    pairs = [(i, i + 1) for i in range(count - 1)]
    if not forward:
        pairs = [(j, i) for i, j in pairs]
    return lax.ppermute(value, TM, pairs)


def ring_shift(value, axis, shift):
    count = lax.axis_size(axis)
    return lax.ppermute(value, axis, [(i, (i + shift) % count) for i in range(count)])


def around_video(rows):
    count = lax.axis_size("video")
    half = rows.shape[0] // 2
    if count != 4:
        held = [rows] + [ring_shift(rows, "video", shift) for shift in range(1, count)]
        return [piece for part in held for piece in (part[:half], part[half:])]
    below, above = ring_shift(rows, "video", 1), ring_shift(rows, "video", 3)
    far = [ring_shift(below[:half], "video", 1), ring_shift(above[half:], "video", 3)]
    return [rows, below] + far + [above]


def exchange(value, axis):
    return lax.all_to_all(value, axis, split_axis=0, concat_axis=0, tiled=True)


def route(first_tap, snip_count, unit_axis):
    count = first_tap[0].shape[0]
    col, row = first_tap
    mine, other = (col, row) if unit_axis == 0 else (row, col)
    reduce_axis = 1 - unit_axis
    block, block_other = mine // snip_count, other // snip_count
    crossing = mine % snip_count == snip_count - 1
    crossing_other = other % snip_count == snip_count - 1
    earlier = lax.broadcasted_iota(jnp.int32, (count, count), reduce_axis) < lax.broadcasted_iota(
        jnp.int32, (count, count), unit_axis
    )
    rank = jnp.sum(
        ((block == block_other) & crossing_other & earlier).astype(jnp.int32),
        axis=reduce_axis,
        keepdims=True,
    )
    target = block + (crossing & (rank % 2 == 1)).astype(jnp.int32)
    return target, mine - target * snip_count


def halved(value):
    high = lax.reduce_precision(value, 8, 7)
    rest = value - high
    middle = lax.reduce_precision(rest, 8, 7)
    return high, middle, rest - middle


def send_slots(bin_grad, tap_weight, tap_index, snip_count, peers):
    video_count, prop_count, bin_count, tap_count = tap_index.shape
    channels = bin_grad.shape[-1]
    units = video_count * prop_count * bin_count
    capacity = bin_count * ((video_count * prop_count + peers - 1) // peers)
    first = tap_index[..., 0].reshape(units)
    taps = (first[:, None], first[None, :])
    target_col, local = route(taps, snip_count, 0)
    target_row, _ = route(taps, snip_count, 1)
    earlier = lax.broadcasted_iota(jnp.int32, (units, units), 0) < lax.broadcasted_iota(
        jnp.int32, (units, units), 1
    )
    position = jnp.sum(
        ((target_col == target_row) & earlier).astype(jnp.int32), axis=0, keepdims=True
    )
    slot = target_row * capacity + position
    matches = (
        lax.broadcasted_iota(jnp.int32, (peers * capacity, units), 0) == slot
    ).astype(jnp.bfloat16)
    video = lax.broadcasted_iota(jnp.int32, (units, 1), 0) // (prop_count * bin_count)
    main = video_count * snip_count

    def line(step):
        at = local + step
        inside = video * snip_count + at
        edge = main + video + jnp.where(at < 0, 0, video_count)
        return jnp.where((at < 0) | (at >= snip_count), edge, inside)

    weights = tap_weight.reshape(units, tap_count)
    columns = []
    for step in range(2):
        where_to = line(step)
        columns += [(where_to // 256).astype(jnp.float32), (where_to % 256).astype(jnp.float32)]
        columns += list(halved(weights[:, step : step + 1]))
    lane = lax.broadcasted_iota(jnp.int32, (units, META), 1)
    meta = jnp.zeros((units, META), jnp.float32)
    for index, column in enumerate(columns):
        meta = jnp.where(lane == index, column, meta)
    payload = jnp.concatenate([bin_grad.reshape(units, channels), meta.astype(jnp.bfloat16)], axis=1)
    rows = jnp.dot(matches, payload, preferred_element_type=jnp.float32).astype(jnp.bfloat16)
    return rows.reshape(peers, capacity, channels + META)


def collect_kernel(grad_ref, meta_ref, out_ref, table_ref):
    meta = meta_ref[...].astype(jnp.float32)

    @pl.when(pl.program_id(0) == 0)
    def _():
        across = meta.T
        row = lax.broadcasted_iota(jnp.int32, table_ref.shape[1:], 0)
        for step in range(2):
            base = 5 * step
            where_to = across[base : base + 1] * 256.0 + across[base + 1 : base + 2]
            hit = row == where_to.astype(jnp.int32)
            table_ref[step] = jnp.where(hit, 1.0, 0.0).astype(jnp.bfloat16)

    grads = grad_ref[...].astype(jnp.float32)
    total = jnp.zeros(out_ref.shape, jnp.float32)
    for step in range(2):
        base = 5 * step + 2
        weight = meta[:, base : base + 1] + meta[:, base + 1 : base + 2] + meta[:, base + 2 : base + 3]
        tap_rows = (weight * grads).astype(jnp.bfloat16)
        total = total + jnp.dot(table_ref[step], tap_rows, preferred_element_type=jnp.float32)
    out_ref[...] = total


def collect(got, channels, row_count):
    rows = got.reshape(-1, channels + META)
    slots = rows.shape[0]
    step = min(256, channels)
    return pl.pallas_call(
        collect_kernel,
        grid=(channels // step,),
        out_shape=jax.ShapeDtypeStruct((row_count, channels), jnp.float32),
        in_specs=[
            pl.BlockSpec((slots, step), lambda q: (0, q)),
            pl.BlockSpec((slots, META), lambda q: (0, channels // META)),
        ],
        out_specs=pl.BlockSpec((row_count, step), lambda q: (0, q)),
        scratch_shapes=[pltpu.VMEM((2, row_count, slots), jnp.bfloat16)],
        compiler_params=pltpu.CompilerParams(vmem_limit_bytes=12 * 2**20),
        cost_estimate=pl.CostEstimate(
            flops=4 * row_count * channels * slots,
            bytes_accessed=5 * 2**20,
            transcendentals=0,
        ),
    )(rows, rows)


def grads_kernel(
    valid_ref,
    part_ref,
    low_in_ref,
    high_in_ref,
    taps_ref,
    pre_ref,
    pre_low_ref,
    pre_high_ref,
    share_ref,
    windows_ref,
):
    videos = low_in_ref.shape[1]
    width = share_ref.shape[3]
    edges = windows_ref.shape[1] - 16
    rows = edges // videos
    channels = part_ref.shape[1]
    quarter = pl.program_id(0)

    @pl.when(quarter == 0)
    def _():
        row = lax.broadcasted_iota(jnp.int32, (rows, channels), 0)
        low_edges, high_edges = ([], [], []), ([], [], [])
        for video in range(videos):
            span = slice(video * rows, (video + 1) * rows)
            one = slice(video, video + 1)
            main = part_ref[span, :]
            main = main + jnp.where(row == 0, low_in_ref[2, one, :], 0.0)
            main = main + jnp.where(row == rows - 1, high_in_ref[0, one, :], 0.0)
            low = part_ref[edges + video : edges + video + 1, :] + low_in_ref[1, one, :]
            high_at = edges + videos + video
            high = part_ref[high_at : high_at + 1, :] + high_in_ref[1, one, :]
            after = jnp.where(row == rows - 1, high, pltpu.roll(main, rows - 1, 0))
            before = jnp.where(row == 0, low, pltpu.roll(main, 1, 0))
            for index, part in enumerate((after, main, before)):
                windows_ref[index, span, :] = part.astype(jnp.bfloat16)
            for index, part in enumerate((main[:1], low, low_in_ref[0, one, :])):
                low_edges[index].append(part)
            for index, part in enumerate((high_in_ref[2, one, :], high, main[rows - 1 :])):
                high_edges[index].append(part)
        spare = [jnp.zeros((windows_ref.shape[1] - edges - 2 * videos, channels), jnp.float32)]
        for index in range(3):
            edge = jnp.concatenate(low_edges[index] + high_edges[index] + spare, axis=0)
            windows_ref[index, edges:, :] = edge.astype(jnp.bfloat16)

    total = jnp.zeros(share_ref.shape[2:], jnp.float32)
    for index in range(3):
        total = total + lax.dot_general(
            windows_ref[index],
            taps_ref[index],
            (((1,), (1,)), ((), ())),
            preferred_element_type=jnp.float32,
        )
    spare = jnp.zeros((windows_ref.shape[1] - edges - 2 * videos, width), jnp.float32)
    slope = jnp.concatenate(
        [
            silu_slope(pre_ref[...].astype(jnp.float32)),
            jnp.where(valid_ref[0] > 0, silu_slope(pre_low_ref[3]), 0.0),
            jnp.where(valid_ref[1] > 0, silu_slope(pre_high_ref[3]), 0.0),
            spare,
        ],
        axis=0,
    )
    share_ref[0, 1] = (total * slope).astype(jnp.bfloat16)
    lanes = pl.ds(pl.multiple_of(quarter * width, width), width)
    share_ref[0, 0] = windows_ref[1, :, lanes]


def gradients(partial, from_low, from_high, filter_second, pre_rows, valid, quarters):
    lag_count, channels, _ = filter_second.shape
    rows, width = pre_rows.shape[0] + 16, channels // quarters
    edge_shape = from_low.shape
    share = jax.ShapeDtypeStruct((quarters, 2, rows, width), jnp.bfloat16)
    share_spec = pl.BlockSpec((1, 2, rows, width), lambda q: (q, 0, 0, 0))
    edge_spec = pl.BlockSpec(edge_shape, lambda q: (0, 0, 0))
    edge_part = pl.BlockSpec(edge_shape[:2] + (width,), lambda q: (0, 0, q))
    return pl.pallas_call(
        grads_kernel,
        grid=(quarters,),
        out_shape=share,
        in_specs=[
            pl.BlockSpec(memory_space=pltpu.SMEM),
            pl.BlockSpec(partial.shape, lambda q: (0, 0)),
            edge_spec,
            edge_spec,
            pl.BlockSpec((lag_count, width, channels), lambda q: (0, q, 0)),
            pl.BlockSpec((pre_rows.shape[0], width), lambda q: (0, q)),
            edge_part,
            edge_part,
        ],
        out_specs=share_spec,
        scratch_shapes=[pltpu.VMEM((lag_count, rows, channels), jnp.bfloat16)],
        compiler_params=pltpu.CompilerParams(vmem_limit_bytes=24 * 2**20),
        cost_estimate=pl.CostEstimate(
            flops=2 * rows * channels * channels * lag_count,
            bytes_accessed=12 * 2**20,
            transcendentals=rows * channels,
        ),
    )(valid, partial, from_low, from_high, filter_second, pre_rows, from_low, from_high)


def terms_kernel(videos, layer, order_ref, grad_ref, *refs):
    input_refs, (keep_ref, give_ref, lag_ref) = refs[:-3], refs[-3:]
    sources, width = grad_ref.shape[0], grad_ref.shape[3]
    main = grad_ref.shape[2] - 16
    rows = main // videos
    _, each, outs = keep_ref.shape
    core = order_ref[0]

    @pl.when(pl.program_id(0) == 0)
    def _():
        row = lax.broadcasted_iota(jnp.int32, (rows, width), 0)
        for source in range(sources):
            at = order_ref[1 + source]
            edges = grad_ref[at, layer, main:, :].astype(jnp.float32)
            for video in range(videos):
                span = slice(video * rows, (video + 1) * rows)
                grad = grad_ref[at, layer, span, :].astype(jnp.float32)
                low, high = edges[video : video + 1], edges[videos + video : videos + video + 1]
                after = jnp.where(row == rows - 1, high, pltpu.roll(grad, rows - 1, 0))
                before = jnp.where(row == 0, low, pltpu.roll(grad, 1, 0))
                for index, part in enumerate((after, grad, before)):
                    lag_ref[
                        source * main + video * rows : source * main + (video + 1) * rows,
                        index * width : (index + 1) * width,
                    ] = part.astype(jnp.bfloat16)

    total = jnp.zeros((input_refs[0].shape[1], outs), jnp.float32)
    offset = 0
    for ref in input_refs:
        total = total + lax.dot_general(
            ref[...],
            lag_ref[offset : offset + ref.shape[0], :],
            (((0,), (0,)), ((), ())),
            preferred_element_type=jnp.float32,
        )
        offset += ref.shape[0]
    total = total.reshape(-1, 2, each, outs)
    first, second = total[:, 0], total[:, 1]
    keep_ref[...] = jnp.where(core == 0, first, second)
    give_ref[...] = jnp.where(core == 0, second, first).astype(jnp.bfloat16)


def filter_terms(inputs, gradients, layer, order, videos, lag_count, each):
    sources, _, block, width = gradients.shape
    channels = inputs[0].shape[-1]
    shape = (channels // (2 * each), each, lag_count * width)
    rows = sources * (block - 16)
    step = min(256, channels)
    out_spec = pl.BlockSpec((step // (2 * each),) + shape[1:], lambda i: (i, 0, 0))
    return pl.pallas_call(
        lambda *refs: terms_kernel(videos, layer, *refs),
        grid=(channels // step,),
        out_shape=(
            jax.ShapeDtypeStruct(shape, jnp.float32),
            jax.ShapeDtypeStruct(shape, jnp.bfloat16),
        ),
        in_specs=[
            pl.BlockSpec(memory_space=pltpu.SMEM),
            pl.BlockSpec(gradients.shape, lambda i: (0, 0, 0, 0)),
        ]
        + [pl.BlockSpec((piece.shape[0], step), lambda i: (0, i)) for piece in inputs],
        out_specs=(out_spec, out_spec),
        scratch_shapes=[pltpu.VMEM((rows, lag_count * width), jnp.bfloat16)],
        compiler_params=pltpu.CompilerParams(vmem_limit_bytes=24 * 2**20),
        cost_estimate=pl.CostEstimate(
            flops=2 * rows * channels * lag_count * width,
            bytes_accessed=10 * 2**20,
            transcendentals=0,
        ),
    )(order, gradients, *inputs)


def share_by_core(keep, give):
    got = ring_shift(give, "core", 1)
    return (keep + got.astype(jnp.float32)).astype(jnp.bfloat16)


def on_device(bin_grad, tap_weight, tap_index, features, preact, filter_second):
    video_count, snip_count, channels = features.shape
    peers = lax.axis_size(TM)
    quarters = lax.axis_size("video")
    place, core = lax.axis_index("video"), lax.axis_index("core")
    lag_count = filter_second.shape[0]
    main_rows = video_count * snip_count
    each = channels // peers
    pre_values = preact.astype(jnp.float32).reshape(main_rows, channels)
    activation = jax.nn.silu(pre_values).astype(jnp.bfloat16)
    sent = send_slots(bin_grad, tap_weight, tap_index, snip_count, peers)
    got = exchange(sent, TM)

    act_all = lax.all_gather(activation, "video", axis=0, tiled=True)
    feature_all = around_video(features.reshape(main_rows, channels))

    partial = collect(got, channels, main_rows + 16)
    ends = partial[:main_rows].reshape(video_count, snip_count, channels)
    low = partial[main_rows : main_rows + video_count]
    high = partial[main_rows + video_count : main_rows + 2 * video_count]
    begun = ((feature_all[1][0, 0] + feature_all[-1][0, 0]) * 0).astype(jnp.float32)
    pre_ends = pre_values.reshape(ends.shape)[:, :: snip_count - 1] + begun
    from_low = neighbours(jnp.stack([ends[:, -2], ends[:, -1], high, pre_ends[:, 1]]), True)
    from_high = neighbours(jnp.stack([low, ends[:, 0], ends[:, 1], pre_ends[:, 0]]), False)
    at = lax.axis_index(TM)
    valid = jnp.stack([at > 0, at < peers - 1]).astype(jnp.int32)
    pre_rows = preact.reshape(main_rows, channels)
    shares = gradients(partial, from_low, from_high, filter_second, pre_rows, valid, quarters)
    block, width = shares.shape[2:]
    shares = exchange(shares.reshape(quarters, 2 * block, width), "video")
    shares = shares.reshape(quarters, 2, block, width)

    in_order = jnp.stack([core] + [jnp.int32(source) for source in range(quarters)])
    around = jnp.stack([core] + [(place + quarters - source) % quarters for source in range(quarters)])
    second = share_by_core(
        *filter_terms([act_all], shares, 0, in_order, video_count, lag_count, each)
    )
    first = share_by_core(
        *filter_terms(feature_all, shares, 1, around, video_count, lag_count, each)
    )
    x_total, z_total = lax.axis_size("x"), lax.axis_size("z")
    both = jnp.stack([part.reshape(x_total, -1, lag_count * width) for part in (first, second)], 1)
    both = exchange(both.reshape(x_total, -1, lag_count * width), "x")
    both = jnp.sum(both.astype(jnp.float32), axis=0).astype(jnp.bfloat16)
    both = both.reshape(2, z_total, each, lag_count * width).transpose(1, 0, 2, 3)
    mine = jnp.sum(exchange(both, "z").astype(jnp.float32), axis=0)

    held = [mine] + [ring_shift(mine, "video", shift) for shift in range(1, quarters)]
    blocks = []
    for quarter in range(quarters):
        block = held[0]
        for shift in range(1, quarters):
            block = jnp.where((place - shift) % quarters == quarter, held[shift], block)
        blocks.append(block.reshape(2, -1, lag_count, width))
    whole = jnp.concatenate(blocks, axis=-1)
    return (whole[0], whole[1])


def solution(mesh):
    shape = (mesh.shape["video"],) + TM_SIZES
    fine = Mesh(np.asarray(mesh.devices).reshape(shape), ("video",) + TM)
    return jax.shard_map(
        on_device,
        mesh=fine,
        in_specs=(
            P("video", TM, None, None),
            P("video", TM, None, None),
            P("video", TM, None, None),
            P("video", TM, None),
            P("video", TM, None),
            P(),
        ),
        out_specs=(P(TM, None, None), P(TM, None, None)),
        check_vma=False,
    )
```

```python
import jax
import jax.numpy as jnp
import numpy as np
from jax import lax
from jax.experimental import pallas as pl
from jax.experimental.pallas import tpu as pltpu
from jax.sharding import Mesh
from jax.sharding import PartitionSpec as P

TM = ("x", "z", "core")
TM_SIZES = (4, 8, 2)
META = 128


def silu_slope(values):
    sigma = jax.nn.sigmoid(values)
    return sigma * (1.0 + values * (1.0 - sigma))


def neighbours(value, forward):
    count = lax.axis_size(TM)
    pairs = [(i, i + 1) for i in range(count - 1)]
    if not forward:
        pairs = [(j, i) for i, j in pairs]
    return lax.ppermute(value, TM, pairs)


def ring_shift(value, axis, shift):
    count = lax.axis_size(axis)
    return lax.ppermute(value, axis, [(i, (i + shift) % count) for i in range(count)])


def exchange(value, axis):
    return lax.all_to_all(value, axis, split_axis=0, concat_axis=0, tiled=True)


def route(first_tap, snip_count, unit_axis):
    count = first_tap[0].shape[0]
    col, row = first_tap
    mine, other = (col, row) if unit_axis == 0 else (row, col)
    reduce_axis = 1 - unit_axis
    block, block_other = mine // snip_count, other // snip_count
    crossing = mine % snip_count == snip_count - 1
    crossing_other = other % snip_count == snip_count - 1
    earlier = lax.broadcasted_iota(jnp.int32, (count, count), reduce_axis) < lax.broadcasted_iota(
        jnp.int32, (count, count), unit_axis
    )
    rank = jnp.sum(
        ((block == block_other) & crossing_other & earlier).astype(jnp.int32),
        axis=reduce_axis,
        keepdims=True,
    )
    target = block + (crossing & (rank % 2 == 1)).astype(jnp.int32)
    return target, mine - target * snip_count


def halved(value):
    high = lax.reduce_precision(value, 8, 7)
    rest = value - high
    middle = lax.reduce_precision(rest, 8, 7)
    return high, middle, rest - middle


def send_slots(bin_grad, tap_weight, tap_index, snip_count, peers):
    video_count, prop_count, bin_count, tap_count = tap_index.shape
    channels = bin_grad.shape[-1]
    units = video_count * prop_count * bin_count
    capacity = bin_count * ((video_count * prop_count + peers - 1) // peers)
    first = tap_index[..., 0].reshape(units)
    taps = (first[:, None], first[None, :])
    target_col, local = route(taps, snip_count, 0)
    target_row, _ = route(taps, snip_count, 1)
    earlier = lax.broadcasted_iota(jnp.int32, (units, units), 0) < lax.broadcasted_iota(
        jnp.int32, (units, units), 1
    )
    position = jnp.sum(
        ((target_col == target_row) & earlier).astype(jnp.int32), axis=0, keepdims=True
    )
    slot = target_row * capacity + position
    matches = (
        lax.broadcasted_iota(jnp.int32, (peers * capacity, units), 0) == slot
    ).astype(jnp.bfloat16)
    video = lax.broadcasted_iota(jnp.int32, (units, 1), 0) // (prop_count * bin_count)
    main = video_count * snip_count

    def line(step):
        at = local + step
        inside = video * snip_count + at
        edge = main + video + jnp.where(at < 0, 0, video_count)
        return jnp.where((at < 0) | (at >= snip_count), edge, inside)

    weights = tap_weight.reshape(units, tap_count)
    columns = []
    for step in range(2):
        where_to = line(step)
        columns += [(where_to // 256).astype(jnp.float32), (where_to % 256).astype(jnp.float32)]
        columns += list(halved(weights[:, step : step + 1]))
    lane = lax.broadcasted_iota(jnp.int32, (units, META), 1)
    meta = jnp.zeros((units, META), jnp.float32)
    for index, column in enumerate(columns):
        meta = jnp.where(lane == index, column, meta)
    payload = jnp.concatenate([bin_grad.reshape(units, channels), meta.astype(jnp.bfloat16)], axis=1)
    rows = jnp.dot(matches, payload, preferred_element_type=jnp.float32).astype(jnp.bfloat16)
    return rows.reshape(peers, capacity, channels + META)


def collect_kernel(grad_ref, meta_ref, out_ref, table_ref):
    meta = meta_ref[...].astype(jnp.float32)

    @pl.when(pl.program_id(0) == 0)
    def _():
        across = meta.T
        row = lax.broadcasted_iota(jnp.int32, table_ref.shape[1:], 0)
        for step in range(2):
            base = 5 * step
            where_to = across[base : base + 1] * 256.0 + across[base + 1 : base + 2]
            hit = row == where_to.astype(jnp.int32)
            table_ref[step] = jnp.where(hit, 1.0, 0.0).astype(jnp.bfloat16)

    grads = grad_ref[...].astype(jnp.float32)
    total = jnp.zeros(out_ref.shape, jnp.float32)
    for step in range(2):
        base = 5 * step + 2
        weight = meta[:, base : base + 1] + meta[:, base + 1 : base + 2] + meta[:, base + 2 : base + 3]
        tap_rows = (weight * grads).astype(jnp.bfloat16)
        total = total + jnp.dot(table_ref[step], tap_rows, preferred_element_type=jnp.float32)
    out_ref[...] = total


def collect(got, channels, row_count):
    rows = got.reshape(-1, channels + META)
    slots = rows.shape[0]
    step = min(256, channels)
    return pl.pallas_call(
        collect_kernel,
        grid=(channels // step,),
        out_shape=jax.ShapeDtypeStruct((row_count, channels), jnp.float32),
        in_specs=[
            pl.BlockSpec((slots, step), lambda q: (0, q)),
            pl.BlockSpec((slots, META), lambda q: (0, channels // META)),
        ],
        out_specs=pl.BlockSpec((row_count, step), lambda q: (0, q)),
        scratch_shapes=[pltpu.VMEM((2, row_count, slots), jnp.bfloat16)],
        compiler_params=pltpu.CompilerParams(vmem_limit_bytes=12 * 2**20),
        cost_estimate=pl.CostEstimate(
            flops=4 * row_count * channels * slots,
            bytes_accessed=5 * 2**20,
            transcendentals=0,
        ),
    )(rows, rows)


def grads_kernel(
    valid_ref,
    part_ref,
    low_in_ref,
    high_in_ref,
    taps_ref,
    pre_ref,
    pre_low_ref,
    pre_high_ref,
    share_ref,
    windows_ref,
):
    videos = low_in_ref.shape[1]
    width = share_ref.shape[3]
    edges = windows_ref.shape[1] - 16
    rows = edges // videos
    channels = part_ref.shape[1]
    quarter = pl.program_id(0)

    @pl.when(quarter == 0)
    def _():
        row = lax.broadcasted_iota(jnp.int32, (rows, channels), 0)
        low_edges, high_edges = ([], [], []), ([], [], [])
        for video in range(videos):
            span = slice(video * rows, (video + 1) * rows)
            one = slice(video, video + 1)
            main = part_ref[span, :]
            main = main + jnp.where(row == 0, low_in_ref[2, one, :], 0.0)
            main = main + jnp.where(row == rows - 1, high_in_ref[0, one, :], 0.0)
            low = part_ref[edges + video : edges + video + 1, :] + low_in_ref[1, one, :]
            high_at = edges + videos + video
            high = part_ref[high_at : high_at + 1, :] + high_in_ref[1, one, :]
            after = jnp.where(row == rows - 1, high, pltpu.roll(main, rows - 1, 0))
            before = jnp.where(row == 0, low, pltpu.roll(main, 1, 0))
            for index, part in enumerate((after, main, before)):
                windows_ref[index, span, :] = part.astype(jnp.bfloat16)
            for index, part in enumerate((main[:1], low, low_in_ref[0, one, :])):
                low_edges[index].append(part)
            for index, part in enumerate((high_in_ref[2, one, :], high, main[rows - 1 :])):
                high_edges[index].append(part)
        spare = [jnp.zeros((windows_ref.shape[1] - edges - 2 * videos, channels), jnp.float32)]
        for index in range(3):
            edge = jnp.concatenate(low_edges[index] + high_edges[index] + spare, axis=0)
            windows_ref[index, edges:, :] = edge.astype(jnp.bfloat16)

    total = jnp.zeros(share_ref.shape[2:], jnp.float32)
    for index in range(3):
        total = total + lax.dot_general(
            windows_ref[index],
            taps_ref[index],
            (((1,), (1,)), ((), ())),
            preferred_element_type=jnp.float32,
        )
    spare = jnp.zeros((windows_ref.shape[1] - edges - 2 * videos, width), jnp.float32)
    slope = jnp.concatenate(
        [
            silu_slope(pre_ref[...].astype(jnp.float32)),
            jnp.where(valid_ref[0] > 0, silu_slope(pre_low_ref[3]), 0.0),
            jnp.where(valid_ref[1] > 0, silu_slope(pre_high_ref[3]), 0.0),
            spare,
        ],
        axis=0,
    )
    share_ref[0, 1] = (total * slope).astype(jnp.bfloat16)
    lanes = pl.ds(pl.multiple_of(quarter * width, width), width)
    share_ref[0, 0] = windows_ref[1, :, lanes]


def gradients(partial, from_low, from_high, filter_second, pre_rows, valid, quarters):
    lag_count, channels, _ = filter_second.shape
    rows, width = pre_rows.shape[0] + 16, channels // quarters
    edge_shape = from_low.shape
    share = jax.ShapeDtypeStruct((quarters, 2, rows, width), jnp.bfloat16)
    share_spec = pl.BlockSpec((1, 2, rows, width), lambda q: (q, 0, 0, 0))
    edge_spec = pl.BlockSpec(edge_shape, lambda q: (0, 0, 0))
    edge_part = pl.BlockSpec(edge_shape[:2] + (width,), lambda q: (0, 0, q))
    return pl.pallas_call(
        grads_kernel,
        grid=(quarters,),
        out_shape=share,
        in_specs=[
            pl.BlockSpec(memory_space=pltpu.SMEM),
            pl.BlockSpec(partial.shape, lambda q: (0, 0)),
            edge_spec,
            edge_spec,
            pl.BlockSpec((lag_count, width, channels), lambda q: (0, q, 0)),
            pl.BlockSpec((pre_rows.shape[0], width), lambda q: (0, q)),
            edge_part,
            edge_part,
        ],
        out_specs=share_spec,
        scratch_shapes=[pltpu.VMEM((lag_count, rows, channels), jnp.bfloat16)],
        compiler_params=pltpu.CompilerParams(vmem_limit_bytes=24 * 2**20),
        cost_estimate=pl.CostEstimate(
            flops=2 * rows * channels * channels * lag_count,
            bytes_accessed=12 * 2**20,
            transcendentals=rows * channels,
        ),
    )(valid, partial, from_low, from_high, filter_second, pre_rows, from_low, from_high)


def terms_kernel(videos, layer, order_ref, grad_ref, *refs):
    input_refs, (keep_ref, give_ref, lag_ref) = refs[:-3], refs[-3:]
    sources, width = grad_ref.shape[0], grad_ref.shape[3]
    main = grad_ref.shape[2] - 16
    rows = main // videos
    _, each, outs = keep_ref.shape
    core = order_ref[0]

    @pl.when(pl.program_id(0) == 0)
    def _():
        row = lax.broadcasted_iota(jnp.int32, (rows, width), 0)
        for source in range(sources):
            at = order_ref[1 + source]
            edges = grad_ref[at, layer, main:, :].astype(jnp.float32)
            for video in range(videos):
                span = slice(video * rows, (video + 1) * rows)
                grad = grad_ref[at, layer, span, :].astype(jnp.float32)
                low, high = edges[video : video + 1], edges[videos + video : videos + video + 1]
                after = jnp.where(row == rows - 1, high, pltpu.roll(grad, rows - 1, 0))
                before = jnp.where(row == 0, low, pltpu.roll(grad, 1, 0))
                for index, part in enumerate((after, grad, before)):
                    lag_ref[
                        source * main + video * rows : source * main + (video + 1) * rows,
                        index * width : (index + 1) * width,
                    ] = part.astype(jnp.bfloat16)

    total = jnp.zeros((input_refs[0].shape[1], outs), jnp.float32)
    offset = 0
    for ref in input_refs:
        total = total + lax.dot_general(
            ref[...],
            lag_ref[offset : offset + ref.shape[0], :],
            (((0,), (0,)), ((), ())),
            preferred_element_type=jnp.float32,
        )
        offset += ref.shape[0]
    total = total.reshape(-1, 2, each, outs)
    first, second = total[:, 0], total[:, 1]
    keep_ref[...] = jnp.where(core == 0, first, second)
    give_ref[...] = jnp.where(core == 0, second, first).astype(jnp.bfloat16)


def filter_terms(inputs, gradients, layer, order, videos, lag_count, each):
    sources, _, block, width = gradients.shape
    channels = inputs[0].shape[-1]
    shape = (channels // (2 * each), each, lag_count * width)
    rows = sources * (block - 16)
    step = min(256, channels)
    out_spec = pl.BlockSpec((step // (2 * each),) + shape[1:], lambda i: (i, 0, 0))
    return pl.pallas_call(
        lambda *refs: terms_kernel(videos, layer, *refs),
        grid=(channels // step,),
        out_shape=(
            jax.ShapeDtypeStruct(shape, jnp.float32),
            jax.ShapeDtypeStruct(shape, jnp.bfloat16),
        ),
        in_specs=[
            pl.BlockSpec(memory_space=pltpu.SMEM),
            pl.BlockSpec(gradients.shape, lambda i: (0, 0, 0, 0)),
        ]
        + [pl.BlockSpec((piece.shape[0], step), lambda i: (0, i)) for piece in inputs],
        out_specs=(out_spec, out_spec),
        scratch_shapes=[pltpu.VMEM((rows, lag_count * width), jnp.bfloat16)],
        compiler_params=pltpu.CompilerParams(vmem_limit_bytes=24 * 2**20),
        cost_estimate=pl.CostEstimate(
            flops=2 * rows * channels * lag_count * width,
            bytes_accessed=10 * 2**20,
            transcendentals=0,
        ),
    )(order, gradients, *inputs)


def share_by_core(keep, give):
    got = ring_shift(give, "core", 1)
    return (keep + got.astype(jnp.float32)).astype(jnp.bfloat16)


def on_device(bin_grad, tap_weight, tap_index, features, preact, filter_second):
    video_count, snip_count, channels = features.shape
    peers = lax.axis_size(TM)
    quarters = lax.axis_size("video")
    place, core = lax.axis_index("video"), lax.axis_index("core")
    lag_count = filter_second.shape[0]
    main_rows = video_count * snip_count
    each = channels // peers
    pre_values = preact.astype(jnp.float32).reshape(main_rows, channels)
    activation = jax.nn.silu(pre_values).astype(jnp.bfloat16)
    sent = send_slots(bin_grad, tap_weight, tap_index, snip_count, peers)
    got = exchange(sent, TM)

    act_all = lax.all_gather(activation, "video", axis=0, tiled=True)
    feature_all = lax.all_gather(
        features.reshape(main_rows, channels), "video", axis=0, tiled=True
    )

    partial = collect(got, channels, main_rows + 16)
    ends = partial[:main_rows].reshape(video_count, snip_count, channels)
    low = partial[main_rows : main_rows + video_count]
    high = partial[main_rows + video_count : main_rows + 2 * video_count]
    pre_ends = pre_values.reshape(ends.shape)[:, :: snip_count - 1]
    from_low = neighbours(jnp.stack([ends[:, -2], ends[:, -1], high, pre_ends[:, 1]]), True)
    from_high = neighbours(jnp.stack([low, ends[:, 0], ends[:, 1], pre_ends[:, 0]]), False)
    at = lax.axis_index(TM)
    valid = jnp.stack([at > 0, at < peers - 1]).astype(jnp.int32)
    pre_rows = preact.reshape(main_rows, channels)
    shares = gradients(partial, from_low, from_high, filter_second, pre_rows, valid, quarters)
    block, width = shares.shape[2:]
    shares = exchange(shares.reshape(quarters, 2 * block, width), "video")
    shares = shares.reshape(quarters, 2, block, width)

    in_order = jnp.stack([core] + [jnp.int32(source) for source in range(quarters)])
    second = share_by_core(
        *filter_terms([act_all], shares, 0, in_order, video_count, lag_count, each)
    )
    first = share_by_core(
        *filter_terms([feature_all], shares, 1, in_order, video_count, lag_count, each)
    )
    x_total, z_total = lax.axis_size("x"), lax.axis_size("z")
    both = jnp.stack([part.reshape(x_total, -1, lag_count * width) for part in (first, second)], 1)
    both = exchange(both.reshape(x_total, -1, lag_count * width), "x")
    both = jnp.sum(both.astype(jnp.float32), axis=0).astype(jnp.bfloat16)
    both = both.reshape(2, z_total, each, lag_count * width).transpose(1, 0, 2, 3)
    mine = jnp.sum(exchange(both, "z").astype(jnp.float32), axis=0)

    held = [mine] + [ring_shift(mine, "video", shift) for shift in range(1, quarters)]
    blocks = []
    for quarter in range(quarters):
        block = held[0]
        for shift in range(1, quarters):
            block = jnp.where((place - shift) % quarters == quarter, held[shift], block)
        blocks.append(block.reshape(2, -1, lag_count, width))
    whole = jnp.concatenate(blocks, axis=-1)
    return (whole[0], whole[1])


def solution(mesh):
    shape = (mesh.shape["video"],) + TM_SIZES
    fine = Mesh(np.asarray(mesh.devices).reshape(shape), ("video",) + TM)
    return jax.shard_map(
        on_device,
        mesh=fine,
        in_specs=(
            P("video", TM, None, None),
            P("video", TM, None, None),
            P("video", TM, None, None),
            P("video", TM, None),
            P("video", TM, None),
            P(),
        ),
        out_specs=(P(TM, None, None), P(TM, None, None)),
        check_vma=False,
    )
```
